32 devices in a mesh: groups: 2 (over y), lon: 4 (over z), lat: 2 (over x), head: 2 (over core).
Axes of the slice: x: 2, y: 2, z: 4, core: 2. Of those that a mesh axis runs over, the one named last changes fastest.
Arguments:
- queries: bfloat16 [4, 4, 128, 1536], P(('groups', 'lat'), 'lon', None, 'head'), parts along dimension 0, may hold values from -12 to 12
- key_tokens: bfloat16 [4, 4, 128, 1536], P(('groups', 'lat'), 'lon', None, 'head'), parts along dimension 0, may hold values from -4 to 4
- value_tokens: bfloat16 [4, 4, 128, 1536], P(('groups', 'lat'), 'lon', None, 'head'), parts along dimension 0, may hold values from -6 to 6
- out_grad: bfloat16 [4, 4, 128, 1536], P(('groups', 'lat'), 'lon', None, 'head'), parts along dimension 0, may hold values from -6 to 6
- counts: int32 [4, 4], P('groups'), parts along dimension 0, may hold values from 16 to 128, as said below
Outputs:
- attended: bfloat16 [4, 4, 128, 1536], P(('groups', 'lat'), 'lon', None, 'head'), parts along dimension 0
- query_grad: bfloat16 [4, 4, 128, 1536], P(('groups', 'lat'), 'lon', None, 'head'), parts along dimension 0
- key_grad: bfloat16 [4, 4, 128, 1536], P(('groups', 'lat'), 'lon', None, 'head'), parts along dimension 0
- value_grad: bfloat16 [4, 4, 128, 1536], P(('groups', 'lat'), 'lon', None, 'head'), parts along dimension 0
The draws below stay inside these ranges and needn't reach their ends.
There are 2 independent parts, one for each index of `groups`. The reference program is written for one: setup_inputs(seed, part) draws one part's arguments, and reference() takes and returns one part's arrays. A program takes and returns all parts, laid end to end along the dimension named above; each array names one. Nothing has to cross between parts.
Inputs may be any that keep to these rules, and one draw needn't show every extreme that they name: `counts`: every row of tiles holds a tile of 128 valid tokens; tiles of the first and last rows hold at least 16 valid tokens, the others at least 64.
All inputs are finite; a program needn't handle non-finite values.
Results may differ from the reference program's by a relative error of at most 0.012.
The reference program's roundings to bfloat16 on the way (of `weights_low` and `grad_scores`) count: a program that leaves them out, or rounds other values in their place, can miss the bound.
Values may be sent and summed in bfloat16 or wider, within the bound.
No kernel may reach another device: no remote copies, remote signals or barrier semaphores. Data moves between devices by JAX's collectives and lax.ppermute only.
A program may use at most 64 MiB of HBM per device.

```python
import math
import jax
import jax.numpy as jnp
from jax import lax

HEADS = 12
HD = 128
TILE = 128
LAT_TILES = 2
LON_TILES = 4
WIDTH = 1536


def draw_queries(key, part):
    arr_shape = (LAT_TILES, LON_TILES, TILE, WIDTH)
    base_draw = jnp.clip(2.0 * jax.random.normal(jax.random.fold_in(key, 1), arr_shape, jnp.float32), -12.0, 12.0)
    return base_draw.astype(jnp.bfloat16)


def draw_key_tokens(key, part):
    arr_shape = (LAT_TILES, LON_TILES, TILE, WIDTH)
    base_draw = jnp.clip(jax.random.normal(jax.random.fold_in(key, 2), arr_shape, jnp.float32), -4.0, 4.0)
    return base_draw.astype(jnp.bfloat16)


def draw_counts(key, part):
    row_ids = jnp.arange(LAT_TILES).reshape(LAT_TILES, 1)
    polar_row = (row_ids == 0) | (row_ids == LAT_TILES - 1)
    lowest = jnp.where(polar_row, TILE // 8, TILE // 2)
    raw_bits = jax.random.randint(jax.random.fold_in(key, 3), (LAT_TILES, LON_TILES), 0, 1 << 20)
    drawn_counts = lowest + raw_bits % (TILE + 1 - lowest)
    full_col = jax.random.randint(jax.random.fold_in(key, 4), (LAT_TILES, 1), 0, LON_TILES)
    col_ids = jnp.arange(LON_TILES).reshape(1, LON_TILES)
    return jnp.where(col_ids == full_col, TILE, drawn_counts).astype(jnp.int32)


def block_levels(own_key, dims, shards, least, top_value):
    gain = 1.0
    for dim, parts in shards:
        steps = jax.random.uniform(jax.random.fold_in(jax.random.fold_in(own_key, 6), dim), (parts,), jnp.float32, least / len(shards), top_value / len(shards))
        gain = gain * jnp.repeat(jnp.exp(steps), dims[dim] // parts).reshape((-1,) + (1,) * (len(dims) - 1 - dim))
    return gain


def bell_draw(key, dims, deviation, reach, cuts=(), kind=jnp.bfloat16):
    result = jax.random.normal(key, dims, jnp.float32) * deviation
    if len(cuts) > 0:
        result = block_levels(key, dims, cuts, -0.22, 0.18) * result
    return jnp.clip(result, min=-reach, max=reach).astype(kind)


def setup_inputs(seed: int = 0, part: int = 0) -> dict:
    keys = jax.random.split(jax.random.key(seed), 6)
    part_splits = jax.random.split(jax.random.fold_in(keys[5], part), 6)
    return {
        "queries": draw_queries(jax.random.fold_in(jax.random.fold_in(keys[5], part), 71), part),
        "key_tokens": draw_key_tokens(jax.random.fold_in(jax.random.fold_in(keys[5], part), 71), part),
        "value_tokens": bell_draw(part_splits[2], (LAT_TILES, LON_TILES, TILE, WIDTH), 1.0, 6.0, ((0, 2), (1, 4), (3, 2))),
        "out_grad": bell_draw(part_splits[3], (LAT_TILES, LON_TILES, TILE, WIDTH), 1.0, 6.0, ((0, 2), (1, 4), (3, 2))),
        "counts": draw_counts(jax.random.fold_in(jax.random.fold_in(keys[5], part), 71), part),
    }


def neighbour_tiles(row_at, col_at):
    row_step = jnp.array([-1, -1, -1, 0, 0, 0, 1, 1, 1], dtype=jnp.int32)
    col_step = jnp.array([-1, 0, 1, -1, 0, 1, -1, 0, 1], dtype=jnp.int32)
    row_next = row_at + row_step
    across = (row_next < 0) | (row_next > LAT_TILES - 1)
    col_next = (col_at + col_step + jnp.where(across, LON_TILES // 2, 0)) % LON_TILES
    row_next = jnp.clip(row_next, 0, LAT_TILES - 1)
    return (row_next * LON_TILES + col_next).astype(jnp.int32)

def reference(queries, key_tokens, value_tokens, out_grad, counts):
    tile_count = LAT_TILES * LON_TILES
    flat_q = queries.reshape(tile_count, TILE, HEADS, HD).astype(jnp.float32)
    flat_k = key_tokens.reshape(tile_count, TILE, HEADS, HD).astype(jnp.float32)
    flat_v = value_tokens.reshape(tile_count, TILE, HEADS, HD).astype(jnp.float32)
    flat_g = out_grad.reshape(tile_count, TILE, HEADS, HD).astype(jnp.float32)
    flat_counts = counts.reshape(-1)
    positions = jnp.arange(TILE, dtype=jnp.int32)
    score_scale = 1.0 / math.sqrt(HD)

    def query_tile(index):
        slot_ids = neighbour_tiles(index // LON_TILES, index % LON_TILES)
        key_valid = (positions[None, :] < flat_counts[slot_ids][:, None]).reshape(-1)
        near_keys = flat_k[slot_ids].reshape(9 * TILE, HEADS, HD)
        near_values = flat_v[slot_ids].reshape(9 * TILE, HEADS, HD)
        query_here = flat_q[index]
        grad_here = flat_g[index]
        scores = jnp.einsum('thd,khd->htk', query_here, near_keys) * score_scale
        row_max = lax.optimization_barrier(jnp.max(jnp.where(key_valid, scores, -1e+30), axis=-1, keepdims=True))
        row_total = lax.optimization_barrier(jnp.sum(jnp.where(key_valid, jnp.exp(scores - row_max), 0.0), axis=-1, keepdims=True))
        log_total = row_max + jnp.log(row_total)
        weights = jnp.where(key_valid, jnp.exp(scores - log_total), 0.0)
        weights_low = lax.optimization_barrier(weights.astype(jnp.bfloat16))
        head_out = jnp.einsum('htk,khd->thd', weights_low.astype(jnp.float32), near_values).astype(jnp.bfloat16)
        head_out = lax.optimization_barrier(head_out)
        out_dot = jnp.einsum('thd,thd->ht', grad_here, head_out.astype(jnp.float32))
        grad_weights = jnp.einsum('thd,khd->htk', grad_here, near_values)
        grad_scores = lax.optimization_barrier((weights * (grad_weights - out_dot[:, :, None])).astype(jnp.bfloat16))
        query_part = (jnp.einsum('htk,khd->thd', grad_scores.astype(jnp.float32), near_keys) * score_scale).astype(jnp.bfloat16)
        return (head_out, query_part, log_total[:, :, 0], out_dot)
    tile_ids = jnp.arange(tile_count, dtype=jnp.int32)
    attended, query_grad, log_totals, out_dots = lax.map(query_tile, tile_ids)

    def key_tile(index):
        slot_ids = neighbour_tiles(index // LON_TILES, index % LON_TILES)
        near_q = flat_q[slot_ids].reshape(9 * TILE, HEADS, HD)
        near_g = flat_g[slot_ids].reshape(9 * TILE, HEADS, HD)
        near_total = jnp.transpose(log_totals[slot_ids], (1, 0, 2)).reshape(HEADS, 9 * TILE)
        near_dot = jnp.transpose(out_dots[slot_ids], (1, 0, 2)).reshape(HEADS, 9 * TILE)
        own_valid = positions < flat_counts[index]
        keys_here = flat_k[index]
        values_here = flat_v[index]
        scores = jnp.einsum('qhd,khd->hqk', near_q, keys_here) * score_scale
        weights = jnp.where(own_valid[None, None, :], jnp.exp(scores - near_total[:, :, None]), 0.0)
        weights_low = lax.optimization_barrier(weights.astype(jnp.bfloat16))
        value_part = jnp.einsum('hqk,qhd->khd', weights_low.astype(jnp.float32), near_g).astype(jnp.bfloat16)
        grad_weights = jnp.einsum('qhd,khd->hqk', near_g, values_here)
        grad_scores = lax.optimization_barrier((weights * (grad_weights - near_dot[:, :, None])).astype(jnp.bfloat16))
        key_part = (jnp.einsum('hqk,qhd->khd', grad_scores.astype(jnp.float32), near_q) * score_scale).astype(jnp.bfloat16)
        return (key_part, value_part)
    key_grad, value_grad = lax.map(key_tile, tile_ids)
    full_shape = (LAT_TILES, LON_TILES, TILE, HEADS * HD)
    return (attended.reshape(full_shape), query_grad.reshape(full_shape), key_grad.reshape(full_shape), value_grad.reshape(full_shape))
```

```python
import functools
import math

import jax
import jax.numpy as jnp
from jax import lax
from jax.experimental import pallas as pl
from jax.experimental.pallas import tpu as pltpu
from jax.sharding import PartitionSpec as P

HD = 128


def with_halo(cells, sides, width, closed):
    for axis, dim in sides:
        count = lax.axis_size(axis)
        ends = count if closed else count - 1
        head = lax.slice_in_dim(cells, 0, width, axis=dim)
        tail = lax.slice_in_dim(cells, cells.shape[dim] - width, cells.shape[dim], axis=dim)
        cells = jnp.concatenate(
            [
                lax.ppermute(tail, axis, [(i, (i + 1) % count) for i in range(ends)]),
                cells,
                lax.ppermute(head, axis, [((i + 1) % count, i) for i in range(ends)]),
            ],
            axis=dim,
        )
    return cells


def passed_along(block, axis, distance):
    devices = range(lax.axis_size(axis))
    route = [((i - distance) % len(devices), i) for i in devices]
    return lax.ppermute(block, axis, route)


def neighbour_tiles(row_at, col_at, lat_tiles, lon_tiles):
    row_step = jnp.array([-1, -1, -1, 0, 0, 0, 1, 1, 1], dtype=jnp.int32)
    col_step = jnp.array([-1, 0, 1, -1, 0, 1, -1, 0, 1], dtype=jnp.int32)
    row_next = row_at + row_step
    across = (row_next < 0) | (row_next > lat_tiles - 1)
    col_next = (col_at + col_step + jnp.where(across, lon_tiles // 2, 0)) % lon_tiles
    row_next = jnp.clip(row_next, 0, lat_tiles - 1)
    return row_next * lon_tiles + col_next


def close_poles(rim_block, mirror):
    lat_index = lax.axis_index("lat")
    last_index = lax.axis_size("lat") - 1
    north_rim = jnp.where(lat_index == 0, mirror, rim_block[:1])
    south_rim = jnp.where(lat_index == last_index, mirror, rim_block[-1:])
    return jnp.concatenate([north_rim, rim_block[1:-1], south_rim], 0)


def around_pair(first_block, second_block):
    row_faces = (
        with_halo(first_block, (("lat", 0),), 1, False),
        with_halo(second_block, (("lat", 0),), 1, False),
    )
    mirror = passed_along((first_block, second_block), "lon", lax.axis_size("lon") // 2)
    column_a = close_poles(row_faces[0], mirror[0])
    column_b = close_poles(row_faces[1], mirror[1])
    return (
        with_halo(column_a, (("lon", 1),), 1, True),
        with_halo(column_b, (("lon", 1),), 1, True),
    )


def around_stats(log_total, out_dot):
    near_stats = (
        with_halo(log_total, (("lon", 1), ("lat", 0)), 1, True),
        with_halo(out_dot, (("lon", 1), ("lat", 0)), 1, True),
    )
    own_rows = log_total.shape[0]
    own_total = near_stats[0][1 : own_rows + 1]
    own_dot = near_stats[1][1 : own_rows + 1]
    mirror = passed_along((own_total, own_dot), "lon", lax.axis_size("lon") // 2)
    return (close_poles(near_stats[0], mirror[0]), close_poles(near_stats[1], mirror[1]))


def by_tiles(queries, key_tokens, value_tokens, out_grad, counts):
    own_rows = queries.shape[0]
    tile_len = queries.shape[2]
    feat_width = queries.shape[3]
    head_count = feat_width // HD
    lat_tiles = counts.shape[0]
    lon_tiles = counts.shape[1]
    row_base = lax.axis_index("lat") * own_rows
    col_at = lax.axis_index("lon")
    score_scale = 1.0 / math.sqrt(HD)
    positions = jnp.arange(tile_len, dtype=jnp.int32)
    flat_counts = counts.reshape(-1)
    near_k, near_v = around_pair(key_tokens, value_tokens)
    slot_ids = neighbour_tiles(row_base, col_at, lat_tiles, lon_tiles)
    key_valid = (positions[None, :] < flat_counts[slot_ids][:, None]).reshape(-1)
    near_keys = near_k.reshape(9 * tile_len, feat_width)
    near_values = near_v.reshape(9 * tile_len, feat_width)
    head_outs = []
    query_parts = []
    head_totals = []
    head_dots = []
    for head_index in range(head_count):
        columns = slice(head_index * HD, (head_index + 1) * HD)
        query_here = queries[0, 0, :, columns]
        grad_here = out_grad[0, 0, :, columns]
        keys_head = near_keys[:, columns]
        values_head = near_values[:, columns]
        scores = (
            jnp.einsum("qd,kd->qk", query_here, keys_head, preferred_element_type=jnp.float32)
            * score_scale
        )
        row_max = jnp.max(jnp.where(key_valid[None, :], scores, -1e30), axis=-1, keepdims=True)
        row_total = jnp.sum(
            jnp.where(key_valid[None, :], jnp.exp(scores - row_max), 0.0), axis=-1, keepdims=True
        )
        log_total = row_max + jnp.log(row_total)
        weights = jnp.where(key_valid[None, :], jnp.exp(scores - log_total), 0.0)
        weights_low = weights.astype(jnp.bfloat16)
        head_out = jnp.dot(weights_low, values_head, preferred_element_type=jnp.float32).astype(
            jnp.bfloat16
        )
        out_dot = jnp.sum(grad_here.astype(jnp.float32) * head_out.astype(jnp.float32), axis=-1)
        grad_weights = jnp.einsum(
            "qd,kd->qk", grad_here, values_head, preferred_element_type=jnp.float32
        )
        grad_scores = (weights * (grad_weights - out_dot[:, None])).astype(jnp.bfloat16)
        query_part = (
            jnp.dot(grad_scores, keys_head, preferred_element_type=jnp.float32) * score_scale
        )
        head_outs.append(head_out)
        query_parts.append(query_part.astype(jnp.bfloat16))
        head_totals.append(log_total[:, 0])
        head_dots.append(out_dot)
    attended = jnp.concatenate(head_outs, -1)[None, None]
    query_grad = jnp.concatenate(query_parts, -1)[None, None]
    own_totals = jnp.stack(head_totals)[None, None]
    own_dots = jnp.stack(head_dots)[None, None]
    near_q, near_g = around_pair(queries, out_grad)
    near_total, near_dot = around_stats(own_totals, own_dots)
    own_valid = positions < counts[row_base, col_at]
    near_queries = near_q.reshape(9 * tile_len, feat_width)
    near_grads = near_g.reshape(9 * tile_len, feat_width)
    key_parts = []
    value_parts = []
    for head_index in range(head_count):
        columns = slice(head_index * HD, (head_index + 1) * HD)
        queries_head = near_queries[:, columns]
        grads_head = near_grads[:, columns]
        keys_here = key_tokens[0, 0, :, columns]
        values_here = value_tokens[0, 0, :, columns]
        totals_head = near_total[:, :, head_index, :].reshape(9 * tile_len)
        dots_head = near_dot[:, :, head_index, :].reshape(9 * tile_len)
        scores = (
            jnp.einsum("qd,kd->qk", queries_head, keys_here, preferred_element_type=jnp.float32)
            * score_scale
        )
        weights = jnp.where(own_valid[None, :], jnp.exp(scores - totals_head[:, None]), 0.0)
        weights_low = weights.astype(jnp.bfloat16)
        value_part = jnp.einsum(
            "qk,qd->kd", weights_low, grads_head, preferred_element_type=jnp.float32
        )
        grad_weights = jnp.einsum(
            "qd,kd->qk", grads_head, values_here, preferred_element_type=jnp.float32
        )
        grad_scores = (weights * (grad_weights - dots_head[:, None])).astype(jnp.bfloat16)
        key_part = (
            jnp.einsum("qk,qd->kd", grad_scores, queries_head, preferred_element_type=jnp.float32)
            * score_scale
        )
        key_parts.append(key_part.astype(jnp.bfloat16))
        value_parts.append(value_part.astype(jnp.bfloat16))
    key_grad = jnp.concatenate(key_parts, -1)[None, None]
    value_grad = jnp.concatenate(value_parts, -1)[None, None]
    return (attended, query_grad, key_grad, value_grad)


def heads_fit(lat, lon, heads):
    fits = (
        heads % lat == 0
        and heads // lat <= lon <= 2 * (heads // lat)
        and lon % 2 == 0
        and 4 <= lat * lon <= 16
    )
    if not fits:
        return False
    first = relative_counts(lat, lon)
    return all(
        relative_counts(lat, lon, row, col, core) == first
        for row in range(lat)
        for col in range(lon)
        for core in range(2)
    )


def relative_counts(lat, lon, row=0, col=0, core=0):
    times = slot_counts(lat, lon)
    tile = []
    for step in steps_of(lat, lon, core):
        from_col = [c for c in range(lon) if column_after(c, step, lon) == col][0]
        tile.append((row - step[1]) % lat * lon + from_col)
    tile = in_slots(tile)
    return [[times[i][j] for j in tile] for i in tile]


def in_slots(found):
    return [*found[:-3], found[-1], *found[-3:-1]]


def in_steps(found):
    return [*found[:-3], *found[-2:], found[-3]]


def head_of(row, col, core, lat, lon, heads):
    per_row = heads // lat
    place = col - (1 - core % 2) * (lon - per_row)
    return row * per_row + place, (place >= 0) & (place < per_row)


def steps_of(lat, lon, core):
    half = lon // 2
    found = [(True, row_step, 0) for row_step in range(lat - 1, -1, -1)]
    for row_step in range(lat - 1, -1, -1):
        for col_step in range(1, half):
            turns = (True, row_step, col_step), (False, row_step, col_step)
            found.extend(turns[::-1] if core % 2 else turns)
    found.extend((False, row_step, 0) for row_step in range(1, lat))
    return found + [(False, 0, 0)]


def column_after(col, step, lon):
    half = lon // 2
    other = col // half ^ int(step[0])
    return other * half + (col + step[2]) % half


def partner(row, col, core, n, lat, lon, back=False):
    places = []
    for which in (0, 1):
        step = steps_of(lat, lon, which)[n]
        to_row = lax.rem(row + (lat - step[1] if back else step[1]), lat)
        to_col = jnp.int32(0)
        for here in range(lon):
            there = column_after(here, step, lon)
            if back:
                to_col = jnp.where(col == there, here, to_col)
            else:
                to_col = jnp.where(col == here, there, to_col)
        places.append((to_row, to_col))
    return [jnp.where(core % 2 == 0, a, b) for a, b in zip(*places)]


def routes(n, lat, lon, cores, heads, back):
    pairs = []
    for row in range(lat):
        for col in range(lon):
            for core in range(cores):
                step = steps_of(lat, lon, core)[n]
                to_row, to_col = (row + step[1]) % lat, column_after(col, step, lon)
                if head_of(to_row, to_col, core, lat, lon, heads)[1]:
                    here = (col * lat + row) * cores + core
                    there = (to_col * lat + to_row) * cores + core
                    pairs.append((there, here) if back else (here, there))
    return pairs


def slot_counts(lat, lon):
    times = [[0] * (lat * lon) for _ in range(lat * lon)]
    for row in range(lat):
        for col in range(lon):
            for a in (-1, 0, 1):
                for b in (-1, 0, 1):
                    near_row, near_col = row + a, col + b
                    if near_row < 0 or near_row > lat - 1:
                        near_col += lon // 2
                        near_row = min(max(near_row, 0), lat - 1)
                    times[row * lon + col][near_row * lon + near_col % lon] += 1
    return times


def pack_kernel(lat, lon, heads, *refs):
    tensors, blocks, whole, sems = refs[:4], refs[4:-2], refs[-2], refs[-1]
    row, col, core = (lax.axis_index(a) for a in ("lat", "lon", "head"))
    parts = sems.shape[1]
    size = whole.shape[1] // parts
    copies = []
    for n in range(parts):
        rows = pl.ds(n * size, size)
        for t, tensor in enumerate(tensors):
            copies.append(
                pltpu.make_async_copy(
                    tensor.at[0, 0, rows, :], whole.at[t, rows, :], sems.at[t, n]
                )
            )
    for copy in copies:
        copy.start()
    for n in range(parts):
        rows = slice(n * size, (n + 1) * size)
        for copy in copies[4 * n : 4 * n + 4]:
            copy.wait()
        for m, block in enumerate(blocks):
            head, used = head_of(*partner(row, col, core, m, lat, lon), core, lat, lon, heads)

            @pl.when(used)
            def _():
                features = pl.ds(pl.multiple_of(head * HD, HD), HD)
                for t in range(4):
                    block[t, rows, :] = whole[t, rows, features]


def unpack_kernel(lat, lon, heads, *refs):
    blocks, tensors, whole, sems = refs[:-6], refs[-6:-2], refs[-2], refs[-1]
    row, col, core = (lax.axis_index(a) for a in ("lat", "lon", "head"))
    parts = sems.shape[1]
    size = whole.shape[1] // parts
    copies = []
    for n in range(parts):
        rows = slice(n * size, (n + 1) * size)
        for m, block in enumerate(blocks):
            head, used = head_of(*partner(row, col, core, m, lat, lon), core, lat, lon, heads)

            @pl.when(used)
            def _():
                features = pl.ds(pl.multiple_of(head * HD, HD), HD)
                for t in range(4):
                    whole[t, rows, features] = block[t, rows, :]

        rows = pl.ds(n * size, size)
        for t, tensor in enumerate(tensors):
            copies.append(
                pltpu.make_async_copy(
                    whole.at[t, rows, :], tensor.at[0, 0, rows, :], sems.at[t, n]
                )
            )
            copies[-1].start()
    for copy in copies:
        copy.wait()


class Sphere:
    def __init__(self, lat, lon, times, key_marks, query_marks):
        self.tiles = lat * lon
        self.times = times
        self.key_marks, self.query_marks = key_marks, query_marks
        self.size = key_marks.shape[1]
        self.wide = 2 * self.size
        self.rounds = self.tiles // 2
        self.scale = 1.0 / math.sqrt(HD)
        self.of_tile = lax.broadcasted_iota(jnp.int32, (1, self.wide), 1) // self.size
        self.held = [None] * self.tiles

    def mark(self, limits):
        shape = (self.size, HD)
        key_row = lax.broadcasted_iota(jnp.int32, shape, 0)
        lane = lax.broadcasted_iota(jnp.int32, shape, 1)
        for j in range(self.tiles):
            unseen = (lane == 0) & (key_row >= limits[j])
            key_mark = jnp.where(unseen, -1e30, jnp.where(lane == j + 1, 1.0, 0.0))
            self.key_marks[j] = key_mark.astype(self.key_marks.dtype)
            apart = jnp.zeros(shape, jnp.bool_)
            for k in range(self.tiles):
                if self.times[j][k] == 0:
                    apart = apart | (lane == k + 1)
            query_mark = jnp.where(apart, -1e30, jnp.where(lane == 0, 1.0, 0.0))
            self.query_marks[j] = query_mark.astype(self.query_marks.dtype)

    def rows(self, j):
        return slice(j * self.size, (j + 1) * self.size)

    def lanes(self, t):
        return slice(t * self.wide, (t + 1) * self.wide)

    def stacked(self, t, n):
        return jnp.concatenate([self.held[2 * t + k][n] for k in range(2)], 0)

    def marked(self, t, n, marks):
        parts = [(self.held[i][n], marks[i]) for i in (2 * t, 2 * t + 1)]
        return jnp.concatenate([jnp.concatenate(part, 1) for part in parts], 0)

    def score(self, t, u):
        return contract_last(
            self.marked(u, 1, self.key_marks), self.marked(t, 0, self.query_marks)
        )

    def grad_weight(self, t, u):
        return contract_last(self.stacked(u, 2), self.stacked(t, 3))

    def exponential(self, scores, top):
        return jnp.exp2((scores - top) * (self.scale * math.log2(math.e)))

    def named(self, t, j):
        line = jnp.ones((1, self.wide), jnp.float32)
        for k in range(2):
            if self.times[2 * t + k][j] > 1:
                line = jnp.where(self.of_tile == k, float(self.times[2 * t + k][j]), line)
        return line

    def folded(self, part, op):
        return op(part.reshape(part.shape[0] // 8, 8, self.wide), axis=0)

    def added(self, total, t, u, parts):
        for k in range(2):
            part = self.folded(parts[self.rows(k), :], jnp.sum) * self.named(t, 2 * u + k)
            total = part if total is None else total + part
        return total


def contract_last(a, b):
    return lax.dot_general(a, b, (((1,), (1,)), ((), ())), preferred_element_type=jnp.float32)


def greater(a, b):
    return b if a is None else jnp.maximum(a, b)


def begin_kernel(lat, lon, times, *refs):
    tiles = lat * lon
    all_counts, blocks, outs = refs[0], refs[1 : tiles - 1], refs[tiles - 1 :]
    key_marks, query_marks, keys_t, values_t, grads_t, scores, grad_weights, stats = outs[:8]
    counts, sem = outs[8:]
    sphere = Sphere(lat, lon, times, key_marks, query_marks)
    sphere.held[: tiles - 2] = blocks
    rounds = sphere.rounds - 1
    copy = pltpu.make_async_copy(all_counts, counts, sem)
    copy.start()
    for t in range(rounds):
        for u in range(rounds):
            grad_weights[t, sphere.lanes(u), :] = sphere.grad_weight(t, u)
        for i in (2 * t, 2 * t + 1):
            keys_t[:, sphere.rows(i)] = blocks[i][1].T
            values_t[:, sphere.rows(i)] = blocks[i][2].T
            grads_t[:, sphere.rows(i)] = blocks[i][3].T
    copy.wait()
    row, col, core = (lax.axis_index(a) for a in ("lat", "lon", "head"))
    limits = [
        counts[tuple(partner(row, col, core, n, lat, lon, True))] for n in range(tiles)
    ]
    sphere.mark(in_slots(limits))
    best, total = [None] * rounds, [None] * rounds

    def score(t, u):
        part = sphere.score(t, u)
        scores[t, sphere.lanes(u), :] = part
        best[t] = greater(best[t], sphere.folded(part, jnp.max))

    for u in range(rounds):
        score(0, u)
    for t in range(rounds):
        best[t] = jnp.max(best[t], axis=0, keepdims=True)
        for u in range(rounds):
            part = sphere.exponential(scores[t, sphere.lanes(u), :], best[t])
            scores[t, sphere.lanes(u), :] = part
            total[t] = sphere.added(total[t], t, u, part)
            if t + 1 < rounds:
                score(t + 1, u)
        stats[t, :8, :] = jnp.broadcast_to(best[t], (8, sphere.wide))
        stats[t, 8:, :] = total[t]


def finish_kernel(lat, lon, times, *refs):
    tiles = lat * lon
    blocks, refs = refs[:tiles], refs[tiles:]
    key_marks, query_marks, keys_t, values_t, grads_t, scores, grad_weights, stats = refs[:8]
    made, refs = refs[8 : 8 + tiles], refs[8 + tiles :]
    last_keys_t, last_values_t, last_grads_t, more_scores, weights_low, grads_low = refs
    sphere = Sphere(lat, lon, times, key_marks, query_marks)
    sphere.held[:] = blocks
    f32, low = jnp.float32, weights_low.dtype
    rounds, last = sphere.rounds, sphere.rounds - 1
    best, total, old, share, out_dot = ([None] * rounds for _ in range(5))
    early = slice(0, last * sphere.wide)
    late = sphere.lanes(last)

    def held_scores(t, j):
        if t < last and j // 2 < last:
            return scores.at[t, sphere.rows(j), :]
        if t < last:
            return more_scores.at[t, sphere.rows(j - 2 * last), :]
        return more_scores.at[last + j // 2, sphere.rows(j % 2), :]

    def score(t, u):
        part = sphere.score(t, u)
        for k in range(2):
            held_scores(t, 2 * u + k)[...] = part[sphere.rows(k), :]
        best[t] = greater(best[t], sphere.folded(part, jnp.max))

    def exponential(t, u):
        parts = []
        for j in (2 * u, 2 * u + 1):
            parts.append(sphere.exponential(held_scores(t, j)[...], best[t]))
            held_scores(t, j)[...] = parts[-1]
        total[t] = sphere.added(total[t], t, u, jnp.concatenate(parts, 0))

    def settle(t):
        before = stats[t, :1, :]
        best[t] = jnp.maximum(before, jnp.max(best[t], axis=0, keepdims=True))
        old[t] = sphere.exponential(before, best[t])
        total[t] = stats[t, 8:, :] * old[t]
        exponential(t, last)
        share[t] = 1.0 / jnp.sum(total[t], axis=0, keepdims=True)

    def factor(t, j):
        line = share[t] * sphere.named(t, j)
        return line * old[t] if t < last and j // 2 < last else line

    def weight(t, u):
        for j in (2 * u, 2 * u + 1):
            part = held_scores(t, j)[...] * factor(t, j)
            weights_low[sphere.rows(j), sphere.lanes(t)] = part.astype(low)

    def from_keys(first_t, last_t, low_scores, t):
        lanes = sphere.lanes(t)
        return jnp.dot(
            first_t[...], low_scores[early, lanes], preferred_element_type=f32
        ) + jnp.dot(last_t[...], low_scores[late, lanes], preferred_element_type=f32)

    def attend(t):
        out_t = from_keys(values_t, last_values_t, weights_low, t).astype(low)
        grad_t = grads_t[:, sphere.lanes(t)] if t < last else last_grads_t[...]
        out_dot[t] = jnp.sum(grad_t.astype(f32) * out_t.astype(f32), axis=0, keepdims=True)
        for k in range(2):
            made[2 * t + k][0] = out_t[:, sphere.rows(k)].T

    def grad_score(t, u):
        if t < last and u < last:
            part = grad_weights[t, sphere.lanes(u), :]
        else:
            part = sphere.grad_weight(t, u)
        for k in range(2):
            j = 2 * u + k
            weights = held_scores(t, j)[...] * factor(t, j)
            grad = weights * (part[sphere.rows(k), :] - out_dot[t])
            grads_low[sphere.rows(j), sphere.lanes(t)] = grad.astype(low)

    def query_grad(t):
        query_t = (from_keys(keys_t, last_keys_t, grads_low, t) * sphere.scale).astype(low)
        for k in range(2):
            made[2 * t + k][1] = query_t[:, sphere.rows(k)].T

    def key_side(n, low_scores, to, factor):
        part = jnp.dot(
            low_scores[...],
            jnp.concatenate([block[n] for block in blocks], 0),
            preferred_element_type=f32,
        )
        for j in range(tiles):
            made[j][to] = (part[sphere.rows(j), :] * factor).astype(low)

    for t in range(last):
        score(t, last)
    for k in range(2):
        block = blocks[2 * last + k]
        last_keys_t[:, sphere.rows(k)] = block[1].T
        last_values_t[:, sphere.rows(k)] = block[2].T
        last_grads_t[:, sphere.rows(k)] = block[3].T
    for t in range(last):
        settle(t)
        if t > 0:
            attend(t - 1)
        if t > 1:
            query_grad(t - 2)
        for u in range(rounds):
            weight(t, u)
            if t == 0:
                score(last, u)
            if t == 1 or last == 1:
                if u == 0:
                    best[last] = jnp.max(best[last], axis=0, keepdims=True)
                exponential(last, u)
            if t > 0:
                grad_score(t - 1, u)
    share[last] = 1.0 / jnp.sum(total[last], axis=0, keepdims=True)
    attend(last - 1)
    if last > 1:
        query_grad(last - 2)
    for u in range(rounds):
        weight(last, u)
        grad_score(last - 1, u)
    attend(last)
    key_side(3, weights_low, 3, 1.0)
    query_grad(last - 1)
    for u in range(rounds):
        grad_score(last, u)
    query_grad(last)
    key_side(0, grads_low, 2, sphere.scale)


def by_heads(queries, key_tokens, value_tokens, out_grad, counts):
    lat, lon, cores = (lax.axis_size(a) for a in ("lat", "lon", "head"))
    tiles = lat * lon
    tile_len, width = queries.shape[2], queries.shape[3]
    heads = width // HD
    low, f32 = queries.dtype, jnp.float32
    in_vmem = pl.BlockSpec(memory_space=pltpu.VMEM)
    in_hbm = pl.BlockSpec(memory_space=pltpu.HBM)
    whole = jax.ShapeDtypeStruct(queries.shape, low)
    block = pltpu.VMEM((4, tile_len, HD), low)
    small = pltpu.CompilerParams(vmem_limit_bytes=6 * 1024 * 1024)

    def sent(blocks, back):
        axes = ("lon", "lat", "head")
        return [
            lax.ppermute(b, axes, routes(n, lat, lon, cores, heads, back))
            for n, b in enumerate(blocks[:-1])
        ] + [blocks[-1]]

    def from_hbm(*arrays):
        return [pltpu.with_memory_space_constraint(x, pltpu.HBM) for x in arrays]

    packed = pl.pallas_call(
        functools.partial(pack_kernel, lat, lon, heads),
        out_shape=[block] * tiles,
        in_specs=[in_hbm] * 4,
        out_specs=[in_vmem] * tiles,
        scratch_shapes=[
            pltpu.VMEM((4, tile_len, width), low),
            pltpu.SemaphoreType.DMA((4, 4)),
        ],
        compiler_params=small,
        name="pack",
    )(*from_hbm(queries, key_tokens, value_tokens, out_grad))
    there = in_slots(sent(packed, False))
    key_len, wide, begun = tiles * tile_len, 2 * tile_len, (tiles - 2) * tile_len
    times = relative_counts(lat, lon)
    large = pltpu.CompilerParams(vmem_limit_bytes=24 * 1024 * 1024)
    shared = [
        pltpu.VMEM((tiles, tile_len, HD), low),
        pltpu.VMEM((tiles, tile_len, HD), low),
        pltpu.VMEM((HD, begun), low),
        pltpu.VMEM((HD, begun), low),
        pltpu.VMEM((HD, begun), low),
        pltpu.VMEM((tiles // 2 - 1, begun, wide), f32),
        pltpu.VMEM((tiles // 2 - 1, begun, wide), f32),
        pltpu.VMEM((tiles // 2 - 1, 16, wide), f32),
    ]
    done = pl.pallas_call(
        functools.partial(begin_kernel, lat, lon, times),
        out_shape=shared,
        in_specs=[in_hbm] + [in_vmem] * (tiles - 2),
        out_specs=[in_vmem] * len(shared),
        scratch_shapes=[pltpu.SMEM(counts.shape, counts.dtype), pltpu.SemaphoreType.DMA],
        compiler_params=large,
        cost_estimate=pl.CostEstimate(
            flops=6 * begun * begun * HD,
            bytes_accessed=8 * begun * HD,
            transcendentals=begun * begun,
        ),
        name="begin",
    )(*from_hbm(counts), *there[: tiles - 2])
    made = pl.pallas_call(
        functools.partial(finish_kernel, lat, lon, times),
        out_shape=[block] * tiles,
        in_specs=[in_vmem] * (tiles + len(shared)),
        out_specs=[in_vmem] * tiles,
        scratch_shapes=[
            pltpu.VMEM((HD, wide), low),
            pltpu.VMEM((HD, wide), low),
            pltpu.VMEM((HD, wide), low),
            pltpu.VMEM((tiles - 1, wide, wide), f32),
            pltpu.VMEM((key_len, key_len), low),
            pltpu.VMEM((key_len, key_len), low),
        ],
        compiler_params=large,
        cost_estimate=pl.CostEstimate(
            flops=14 * key_len * key_len * HD - 6 * begun * begun * HD,
            bytes_accessed=16 * key_len * HD,
            transcendentals=key_len * key_len - begun * begun,
        ),
        name="finish",
    )(*there, *done)
    home = sent(in_steps(made), True)
    return tuple(
        pl.pallas_call(
            functools.partial(unpack_kernel, lat, lon, heads),
            out_shape=[whole] * 4,
            in_specs=[in_vmem] * tiles,
            out_specs=[in_hbm] * 4,
            scratch_shapes=[
                pltpu.VMEM((4, tile_len, width), low),
                pltpu.SemaphoreType.DMA((4, 4)),
            ],
            compiler_params=small,
            name="unpack",
        )(*home)
    )


def solution(mesh):
    tokens = P(("groups", "lat"), "lon", None, "head")

    def on_device(queries, *rest):
        lat, lon = mesh.shape["lat"], mesh.shape["lon"]
        one_tile = queries.shape[:2] == (1, 1)
        if one_tile and heads_fit(lat, lon, queries.shape[3] // HD):
            return by_heads(queries, *rest)
        return by_tiles(queries, *rest)

    return jax.shard_map(
        on_device,
        mesh=mesh,
        in_specs=(tokens,) * 4 + (P("groups", None),),
        out_specs=(tokens,) * 4,
        check_vma=False,
    )
```

```python
import functools
import math

import jax
import jax.numpy as jnp
from jax import lax
from jax.experimental import pallas as pl
from jax.experimental.pallas import tpu as pltpu
from jax.sharding import PartitionSpec as P

HD = 128


def with_halo(cells, sides, width, closed):
    for axis, dim in sides:
        count = lax.axis_size(axis)
        ends = count if closed else count - 1
        head = lax.slice_in_dim(cells, 0, width, axis=dim)
        tail = lax.slice_in_dim(cells, cells.shape[dim] - width, cells.shape[dim], axis=dim)
        cells = jnp.concatenate(
            [
                lax.ppermute(tail, axis, [(i, (i + 1) % count) for i in range(ends)]),
                cells,
                lax.ppermute(head, axis, [((i + 1) % count, i) for i in range(ends)]),
            ],
            axis=dim,
        )
    return cells


def passed_along(block, axis, distance):
    devices = range(lax.axis_size(axis))
    route = [((i - distance) % len(devices), i) for i in devices]
    return lax.ppermute(block, axis, route)


def neighbour_tiles(row_at, col_at, lat_tiles, lon_tiles):
    row_step = jnp.array([-1, -1, -1, 0, 0, 0, 1, 1, 1], dtype=jnp.int32)
    col_step = jnp.array([-1, 0, 1, -1, 0, 1, -1, 0, 1], dtype=jnp.int32)
    row_next = row_at + row_step
    across = (row_next < 0) | (row_next > lat_tiles - 1)
    col_next = (col_at + col_step + jnp.where(across, lon_tiles // 2, 0)) % lon_tiles
    row_next = jnp.clip(row_next, 0, lat_tiles - 1)
    return row_next * lon_tiles + col_next


def close_poles(rim_block, mirror):
    lat_index = lax.axis_index("lat")
    last_index = lax.axis_size("lat") - 1
    north_rim = jnp.where(lat_index == 0, mirror, rim_block[:1])
    south_rim = jnp.where(lat_index == last_index, mirror, rim_block[-1:])
    return jnp.concatenate([north_rim, rim_block[1:-1], south_rim], 0)


def around_pair(first_block, second_block):
    row_faces = (
        with_halo(first_block, (("lat", 0),), 1, False),
        with_halo(second_block, (("lat", 0),), 1, False),
    )
    mirror = passed_along((first_block, second_block), "lon", lax.axis_size("lon") // 2)
    column_a = close_poles(row_faces[0], mirror[0])
    column_b = close_poles(row_faces[1], mirror[1])
    return (
        with_halo(column_a, (("lon", 1),), 1, True),
        with_halo(column_b, (("lon", 1),), 1, True),
    )


def around_stats(log_total, out_dot):
    near_stats = (
        with_halo(log_total, (("lon", 1), ("lat", 0)), 1, True),
        with_halo(out_dot, (("lon", 1), ("lat", 0)), 1, True),
    )
    own_rows = log_total.shape[0]
    own_total = near_stats[0][1 : own_rows + 1]
    own_dot = near_stats[1][1 : own_rows + 1]
    mirror = passed_along((own_total, own_dot), "lon", lax.axis_size("lon") // 2)
    return (close_poles(near_stats[0], mirror[0]), close_poles(near_stats[1], mirror[1]))


def by_tiles(queries, key_tokens, value_tokens, out_grad, counts):
    own_rows = queries.shape[0]
    tile_len = queries.shape[2]
    feat_width = queries.shape[3]
    head_count = feat_width // HD
    lat_tiles = counts.shape[0]
    lon_tiles = counts.shape[1]
    row_base = lax.axis_index("lat") * own_rows
    col_at = lax.axis_index("lon")
    score_scale = 1.0 / math.sqrt(HD)
    positions = jnp.arange(tile_len, dtype=jnp.int32)
    flat_counts = counts.reshape(-1)
    near_k, near_v = around_pair(key_tokens, value_tokens)
    slot_ids = neighbour_tiles(row_base, col_at, lat_tiles, lon_tiles)
    key_valid = (positions[None, :] < flat_counts[slot_ids][:, None]).reshape(-1)
    near_keys = near_k.reshape(9 * tile_len, feat_width)
    near_values = near_v.reshape(9 * tile_len, feat_width)
    head_outs = []
    query_parts = []
    head_totals = []
    head_dots = []
    for head_index in range(head_count):
        columns = slice(head_index * HD, (head_index + 1) * HD)
        query_here = queries[0, 0, :, columns]
        grad_here = out_grad[0, 0, :, columns]
        keys_head = near_keys[:, columns]
        values_head = near_values[:, columns]
        scores = (
            jnp.einsum("qd,kd->qk", query_here, keys_head, preferred_element_type=jnp.float32)
            * score_scale
        )
        row_max = jnp.max(jnp.where(key_valid[None, :], scores, -1e30), axis=-1, keepdims=True)
        row_total = jnp.sum(
            jnp.where(key_valid[None, :], jnp.exp(scores - row_max), 0.0), axis=-1, keepdims=True
        )
        log_total = row_max + jnp.log(row_total)
        weights = jnp.where(key_valid[None, :], jnp.exp(scores - log_total), 0.0)
        weights_low = weights.astype(jnp.bfloat16)
        head_out = jnp.dot(weights_low, values_head, preferred_element_type=jnp.float32).astype(
            jnp.bfloat16
        )
        out_dot = jnp.sum(grad_here.astype(jnp.float32) * head_out.astype(jnp.float32), axis=-1)
        grad_weights = jnp.einsum(
            "qd,kd->qk", grad_here, values_head, preferred_element_type=jnp.float32
        )
        grad_scores = (weights * (grad_weights - out_dot[:, None])).astype(jnp.bfloat16)
        query_part = (
            jnp.dot(grad_scores, keys_head, preferred_element_type=jnp.float32) * score_scale
        )
        head_outs.append(head_out)
        query_parts.append(query_part.astype(jnp.bfloat16))
        head_totals.append(log_total[:, 0])
        head_dots.append(out_dot)
    attended = jnp.concatenate(head_outs, -1)[None, None]
    query_grad = jnp.concatenate(query_parts, -1)[None, None]
    own_totals = jnp.stack(head_totals)[None, None]
    own_dots = jnp.stack(head_dots)[None, None]
    near_q, near_g = around_pair(queries, out_grad)
    near_total, near_dot = around_stats(own_totals, own_dots)
    own_valid = positions < counts[row_base, col_at]
    near_queries = near_q.reshape(9 * tile_len, feat_width)
    near_grads = near_g.reshape(9 * tile_len, feat_width)
    key_parts = []
    value_parts = []
    for head_index in range(head_count):
        columns = slice(head_index * HD, (head_index + 1) * HD)
        queries_head = near_queries[:, columns]
        grads_head = near_grads[:, columns]
        keys_here = key_tokens[0, 0, :, columns]
        values_here = value_tokens[0, 0, :, columns]
        totals_head = near_total[:, :, head_index, :].reshape(9 * tile_len)
        dots_head = near_dot[:, :, head_index, :].reshape(9 * tile_len)
        scores = (
            jnp.einsum("qd,kd->qk", queries_head, keys_here, preferred_element_type=jnp.float32)
            * score_scale
        )
        weights = jnp.where(own_valid[None, :], jnp.exp(scores - totals_head[:, None]), 0.0)
        weights_low = weights.astype(jnp.bfloat16)
        value_part = jnp.einsum(
            "qk,qd->kd", weights_low, grads_head, preferred_element_type=jnp.float32
        )
        grad_weights = jnp.einsum(
            "qd,kd->qk", grads_head, values_here, preferred_element_type=jnp.float32
        )
        grad_scores = (weights * (grad_weights - dots_head[:, None])).astype(jnp.bfloat16)
        key_part = (
            jnp.einsum("qk,qd->kd", grad_scores, queries_head, preferred_element_type=jnp.float32)
            * score_scale
        )
        key_parts.append(key_part.astype(jnp.bfloat16))
        value_parts.append(value_part.astype(jnp.bfloat16))
    key_grad = jnp.concatenate(key_parts, -1)[None, None]
    value_grad = jnp.concatenate(value_parts, -1)[None, None]
    return (attended, query_grad, key_grad, value_grad)


def heads_fit(lat, lon, heads):
    fits = (
        heads % lat == 0
        and heads // lat <= lon <= 2 * (heads // lat)
        and lon % 2 == 0
        and 4 <= lat * lon <= 16
    )
    if not fits:
        return False
    first = relative_counts(lat, lon)
    return all(
        relative_counts(lat, lon, row, col, core) == first
        for row in range(lat)
        for col in range(lon)
        for core in range(2)
    )


def relative_counts(lat, lon, row=0, col=0, core=0):
    times = slot_counts(lat, lon)
    tile = []
    for step in steps_of(lat, lon, core):
        from_col = [c for c in range(lon) if column_after(c, step, lon) == col][0]
        tile.append((row - step[1]) % lat * lon + from_col)
    tile = in_slots(tile)
    return [[times[i][j] for j in tile] for i in tile]


def in_slots(found):
    return [*found[:-3], found[-1], *found[-3:-1]]


def in_steps(found):
    return [*found[:-3], *found[-2:], found[-3]]


def head_of(row, col, core, lat, lon, heads):
    per_row = heads // lat
    place = col - (1 - core % 2) * (lon - per_row)
    return row * per_row + place, (place >= 0) & (place < per_row)


def steps_of(lat, lon, core):
    half = lon // 2
    found = [(True, row_step, 0) for row_step in range(lat - 1, -1, -1)]
    for row_step in range(lat - 1, -1, -1):
        for col_step in range(1, half):
            turns = (True, row_step, col_step), (False, row_step, col_step)
            found.extend(turns if core % 2 else turns[::-1])
    found.extend((False, row_step, 0) for row_step in range(1, lat))
    return found + [(False, 0, 0)]


def column_after(col, step, lon):
    half = lon // 2
    other = col // half ^ int(step[0])
    return other * half + (col + step[2]) % half


def partner(row, col, core, n, lat, lon, back=False):
    places = []
    for which in (0, 1):
        step = steps_of(lat, lon, which)[n]
        to_row = lax.rem(row + (lat - step[1] if back else step[1]), lat)
        to_col = jnp.int32(0)
        for here in range(lon):
            there = column_after(here, step, lon)
            if back:
                to_col = jnp.where(col == there, here, to_col)
            else:
                to_col = jnp.where(col == here, there, to_col)
        places.append((to_row, to_col))
    return [jnp.where(core % 2 == 0, a, b) for a, b in zip(*places)]


def routes(n, lat, lon, cores, heads, back):
    pairs = []
    for row in range(lat):
        for col in range(lon):
            for core in range(cores):
                step = steps_of(lat, lon, core)[n]
                to_row, to_col = (row + step[1]) % lat, column_after(col, step, lon)
                if head_of(to_row, to_col, core, lat, lon, heads)[1]:
                    here = (col * lat + row) * cores + core
                    there = (to_col * lat + to_row) * cores + core
                    pairs.append((there, here) if back else (here, there))
    return pairs


def slot_counts(lat, lon):
    times = [[0] * (lat * lon) for _ in range(lat * lon)]
    for row in range(lat):
        for col in range(lon):
            for a in (-1, 0, 1):
                for b in (-1, 0, 1):
                    near_row, near_col = row + a, col + b
                    if near_row < 0 or near_row > lat - 1:
                        near_col += lon // 2
                        near_row = min(max(near_row, 0), lat - 1)
                    times[row * lon + col][near_row * lon + near_col % lon] += 1
    return times


def pack_kernel(lat, lon, heads, *refs):
    tensors, blocks, whole, sems = refs[:4], refs[4:-2], refs[-2], refs[-1]
    row, col, core = (lax.axis_index(a) for a in ("lat", "lon", "head"))
    parts = sems.shape[1]
    size = whole.shape[1] // parts
    copies = []
    for n in range(parts):
        rows = pl.ds(n * size, size)
        for t, tensor in enumerate(tensors):
            copies.append(
                pltpu.make_async_copy(
                    tensor.at[0, 0, rows, :], whole.at[t, rows, :], sems.at[t, n]
                )
            )
    for copy in copies:
        copy.start()
    for n in range(parts):
        rows = slice(n * size, (n + 1) * size)
        for copy in copies[4 * n : 4 * n + 4]:
            copy.wait()
        for m, block in enumerate(blocks):
            head, used = head_of(*partner(row, col, core, m, lat, lon), core, lat, lon, heads)

            @pl.when(used)
            def _():
                features = pl.ds(pl.multiple_of(head * HD, HD), HD)
                for t in range(4):
                    block[t, rows, :] = whole[t, rows, features]


def unpack_kernel(lat, lon, heads, *refs):
    blocks, tensors, whole, sems = refs[:-6], refs[-6:-2], refs[-2], refs[-1]
    row, col, core = (lax.axis_index(a) for a in ("lat", "lon", "head"))
    parts = sems.shape[1]
    size = whole.shape[1] // parts
    copies = []
    for n in range(parts):
        rows = slice(n * size, (n + 1) * size)
        for m, block in enumerate(blocks):
            head, used = head_of(*partner(row, col, core, m, lat, lon), core, lat, lon, heads)

            @pl.when(used)
            def _():
                features = pl.ds(pl.multiple_of(head * HD, HD), HD)
                for t in range(4):
                    whole[t, rows, features] = block[t, rows, :]

        rows = pl.ds(n * size, size)
        for t, tensor in enumerate(tensors):
            copies.append(
                pltpu.make_async_copy(
                    whole.at[t, rows, :], tensor.at[0, 0, rows, :], sems.at[t, n]
                )
            )
            copies[-1].start()
    for copy in copies:
        copy.wait()


class Sphere:
    def __init__(self, lat, lon, times, key_marks, query_marks):
        self.tiles = lat * lon
        self.times = times
        self.key_marks, self.query_marks = key_marks, query_marks
        self.size = key_marks.shape[1]
        self.wide = 2 * self.size
        self.rounds = self.tiles // 2
        self.scale = 1.0 / math.sqrt(HD)
        self.of_tile = lax.broadcasted_iota(jnp.int32, (1, self.wide), 1) // self.size
        self.held = [None] * self.tiles

    def mark(self, limits):
        shape = (self.size, HD)
        key_row = lax.broadcasted_iota(jnp.int32, shape, 0)
        lane = lax.broadcasted_iota(jnp.int32, shape, 1)
        for j in range(self.tiles):
            unseen = (lane == 0) & (key_row >= limits[j])
            key_mark = jnp.where(unseen, -1e30, jnp.where(lane == j + 1, 1.0, 0.0))
            self.key_marks[j] = key_mark.astype(self.key_marks.dtype)
            apart = jnp.zeros(shape, jnp.bool_)
            for k in range(self.tiles):
                if self.times[j][k] == 0:
                    apart = apart | (lane == k + 1)
            query_mark = jnp.where(apart, -1e30, jnp.where(lane == 0, 1.0, 0.0))
            self.query_marks[j] = query_mark.astype(self.query_marks.dtype)

    def rows(self, j):
        return slice(j * self.size, (j + 1) * self.size)

    def lanes(self, t):
        return slice(t * self.wide, (t + 1) * self.wide)

    def stacked(self, t, n):
        return jnp.concatenate([self.held[2 * t + k][n] for k in range(2)], 0)

    def marked(self, t, n, marks):
        parts = [(self.held[i][n], marks[i]) for i in (2 * t, 2 * t + 1)]
        return jnp.concatenate([jnp.concatenate(part, 1) for part in parts], 0)

    def score(self, t, u):
        return contract_last(
            self.marked(u, 1, self.key_marks), self.marked(t, 0, self.query_marks)
        )

    def grad_weight(self, t, u):
        return contract_last(self.stacked(u, 2), self.stacked(t, 3))

    def exponential(self, scores, top):
        return jnp.exp2((scores - top) * (self.scale * math.log2(math.e)))

    def named(self, t, j):
        line = jnp.ones((1, self.wide), jnp.float32)
        for k in range(2):
            if self.times[2 * t + k][j] > 1:
                line = jnp.where(self.of_tile == k, float(self.times[2 * t + k][j]), line)
        return line

    def folded(self, part, op):
        return op(part.reshape(part.shape[0] // 8, 8, self.wide), axis=0)

    def added(self, total, t, u, parts):
        for k in range(2):
            part = self.folded(parts[self.rows(k), :], jnp.sum) * self.named(t, 2 * u + k)
            total = part if total is None else total + part
        return total


def contract_last(a, b):
    return lax.dot_general(a, b, (((1,), (1,)), ((), ())), preferred_element_type=jnp.float32)


def greater(a, b):
    return b if a is None else jnp.maximum(a, b)


def begin_kernel(lat, lon, times, *refs):
    tiles = lat * lon
    all_counts, blocks, outs = refs[0], refs[1 : tiles - 1], refs[tiles - 1 :]
    key_marks, query_marks, keys_t, values_t, grads_t, scores, grad_weights, stats = outs[:8]
    counts, sem = outs[8:]
    sphere = Sphere(lat, lon, times, key_marks, query_marks)
    sphere.held[: tiles - 2] = blocks
    rounds = sphere.rounds - 1
    copy = pltpu.make_async_copy(all_counts, counts, sem)
    copy.start()
    for t in range(rounds):
        for u in range(rounds):
            grad_weights[t, sphere.lanes(u), :] = sphere.grad_weight(t, u)
        for i in (2 * t, 2 * t + 1):
            keys_t[:, sphere.rows(i)] = blocks[i][1].T
            values_t[:, sphere.rows(i)] = blocks[i][2].T
            grads_t[:, sphere.rows(i)] = blocks[i][3].T
    copy.wait()
    row, col, core = (lax.axis_index(a) for a in ("lat", "lon", "head"))
    limits = [
        counts[tuple(partner(row, col, core, n, lat, lon, True))] for n in range(tiles)
    ]
    sphere.mark(in_slots(limits))
    best, total = [None] * rounds, [None] * rounds

    def score(t, u):
        part = sphere.score(t, u)
        scores[t, sphere.lanes(u), :] = part
        best[t] = greater(best[t], sphere.folded(part, jnp.max))

    for u in range(rounds):
        score(0, u)
    for t in range(rounds):
        best[t] = jnp.max(best[t], axis=0, keepdims=True)
        for u in range(rounds):
            part = sphere.exponential(scores[t, sphere.lanes(u), :], best[t])
            scores[t, sphere.lanes(u), :] = part
            total[t] = sphere.added(total[t], t, u, part)
            if t + 1 < rounds:
                score(t + 1, u)
        stats[t, :8, :] = jnp.broadcast_to(best[t], (8, sphere.wide))
        stats[t, 8:, :] = total[t]


def finish_kernel(lat, lon, times, *refs):
    tiles = lat * lon
    blocks, refs = refs[:tiles], refs[tiles:]
    key_marks, query_marks, keys_t, values_t, grads_t, scores, grad_weights, stats = refs[:8]
    made, refs = refs[8 : 8 + tiles], refs[8 + tiles :]
    last_keys_t, last_values_t, last_grads_t, more_scores, weights_low, grads_low = refs
    sphere = Sphere(lat, lon, times, key_marks, query_marks)
    sphere.held[:] = blocks
    f32, low = jnp.float32, weights_low.dtype
    rounds, last = sphere.rounds, sphere.rounds - 1
    best, total, old, share, out_dot = ([None] * rounds for _ in range(5))
    early = slice(0, last * sphere.wide)
    late = sphere.lanes(last)

    def held_scores(t, j):
        if t < last and j // 2 < last:
            return scores.at[t, sphere.rows(j), :]
        if t < last:
            return more_scores.at[t, sphere.rows(j - 2 * last), :]
        return more_scores.at[last + j // 2, sphere.rows(j % 2), :]

    def score(t, u):
        part = sphere.score(t, u)
        for k in range(2):
            held_scores(t, 2 * u + k)[...] = part[sphere.rows(k), :]
        best[t] = greater(best[t], sphere.folded(part, jnp.max))

    def exponential(t, u):
        parts = []
        for j in (2 * u, 2 * u + 1):
            parts.append(sphere.exponential(held_scores(t, j)[...], best[t]))
            held_scores(t, j)[...] = parts[-1]
        total[t] = sphere.added(total[t], t, u, jnp.concatenate(parts, 0))

    def settle(t):
        before = stats[t, :1, :]
        best[t] = jnp.maximum(before, jnp.max(best[t], axis=0, keepdims=True))
        old[t] = sphere.exponential(before, best[t])
        total[t] = stats[t, 8:, :] * old[t]
        exponential(t, last)
        share[t] = 1.0 / jnp.sum(total[t], axis=0, keepdims=True)

    def factor(t, j):
        line = share[t] * sphere.named(t, j)
        return line * old[t] if t < last and j // 2 < last else line

    def weight(t, u):
        for j in (2 * u, 2 * u + 1):
            part = held_scores(t, j)[...] * factor(t, j)
            weights_low[sphere.rows(j), sphere.lanes(t)] = part.astype(low)

    def from_keys(first_t, last_t, low_scores, t):
        lanes = sphere.lanes(t)
        return jnp.dot(
            first_t[...], low_scores[early, lanes], preferred_element_type=f32
        ) + jnp.dot(last_t[...], low_scores[late, lanes], preferred_element_type=f32)

    def attend(t):
        out_t = from_keys(values_t, last_values_t, weights_low, t).astype(low)
        grad_t = grads_t[:, sphere.lanes(t)] if t < last else last_grads_t[...]
        out_dot[t] = jnp.sum(grad_t.astype(f32) * out_t.astype(f32), axis=0, keepdims=True)
        for k in range(2):
            made[2 * t + k][0] = out_t[:, sphere.rows(k)].T

    def grad_score(t, u):
        if t < last and u < last:
            part = grad_weights[t, sphere.lanes(u), :]
        else:
            part = sphere.grad_weight(t, u)
        for k in range(2):
            j = 2 * u + k
            weights = held_scores(t, j)[...] * factor(t, j)
            grad = weights * (part[sphere.rows(k), :] - out_dot[t])
            grads_low[sphere.rows(j), sphere.lanes(t)] = grad.astype(low)

    def query_grad(t):
        query_t = (from_keys(keys_t, last_keys_t, grads_low, t) * sphere.scale).astype(low)
        for k in range(2):
            made[2 * t + k][1] = query_t[:, sphere.rows(k)].T

    def key_side(n, low_scores, to, factor):
        part = jnp.dot(
            low_scores[...],
            jnp.concatenate([block[n] for block in blocks], 0),
            preferred_element_type=f32,
        )
        for j in range(tiles):
            made[j][to] = (part[sphere.rows(j), :] * factor).astype(low)

    for t in range(last):
        score(t, last)
    for k in range(2):
        block = blocks[2 * last + k]
        last_keys_t[:, sphere.rows(k)] = block[1].T
        last_values_t[:, sphere.rows(k)] = block[2].T
        last_grads_t[:, sphere.rows(k)] = block[3].T
    for t in range(last):
        settle(t)
        if t > 0:
            attend(t - 1)
        if t > 1:
            query_grad(t - 2)
        for u in range(rounds):
            weight(t, u)
            if t == 0:
                score(last, u)
            if t == 1 or last == 1:
                if u == 0:
                    best[last] = jnp.max(best[last], axis=0, keepdims=True)
                exponential(last, u)
            if t > 0:
                grad_score(t - 1, u)
    share[last] = 1.0 / jnp.sum(total[last], axis=0, keepdims=True)
    attend(last - 1)
    if last > 1:
        query_grad(last - 2)
    for u in range(rounds):
        weight(last, u)
        grad_score(last - 1, u)
    attend(last)
    key_side(3, weights_low, 3, 1.0)
    query_grad(last - 1)
    for u in range(rounds):
        grad_score(last, u)
    query_grad(last)
    key_side(0, grads_low, 2, sphere.scale)


def by_heads(queries, key_tokens, value_tokens, out_grad, counts):
    lat, lon, cores = (lax.axis_size(a) for a in ("lat", "lon", "head"))
    tiles = lat * lon
    tile_len, width = queries.shape[2], queries.shape[3]
    heads = width // HD
    low, f32 = queries.dtype, jnp.float32
    in_vmem = pl.BlockSpec(memory_space=pltpu.VMEM)
    in_hbm = pl.BlockSpec(memory_space=pltpu.HBM)
    whole = jax.ShapeDtypeStruct(queries.shape, low)
    block = pltpu.VMEM((4, tile_len, HD), low)
    small = pltpu.CompilerParams(vmem_limit_bytes=6 * 1024 * 1024)

    def sent(blocks, back):
        axes = ("lon", "lat", "head")
        return [
            lax.ppermute(b, axes, routes(n, lat, lon, cores, heads, back))
            for n, b in enumerate(blocks[:-1])
        ] + [blocks[-1]]

    def from_hbm(*arrays):
        return [pltpu.with_memory_space_constraint(x, pltpu.HBM) for x in arrays]

    packed = pl.pallas_call(
        functools.partial(pack_kernel, lat, lon, heads),
        out_shape=[block] * tiles,
        in_specs=[in_hbm] * 4,
        out_specs=[in_vmem] * tiles,
        scratch_shapes=[
            pltpu.VMEM((4, tile_len, width), low),
            pltpu.SemaphoreType.DMA((4, 4)),
        ],
        compiler_params=small,
        name="pack",
    )(*from_hbm(queries, key_tokens, value_tokens, out_grad))
    there = in_slots(sent(packed, False))
    key_len, wide, begun = tiles * tile_len, 2 * tile_len, (tiles - 2) * tile_len
    times = relative_counts(lat, lon)
    large = pltpu.CompilerParams(vmem_limit_bytes=24 * 1024 * 1024)
    shared = [
        pltpu.VMEM((tiles, tile_len, HD), low),
        pltpu.VMEM((tiles, tile_len, HD), low),
        pltpu.VMEM((HD, begun), low),
        pltpu.VMEM((HD, begun), low),
        pltpu.VMEM((HD, begun), low),
        pltpu.VMEM((tiles // 2 - 1, begun, wide), f32),
        pltpu.VMEM((tiles // 2 - 1, begun, wide), f32),
        pltpu.VMEM((tiles // 2 - 1, 16, wide), f32),
    ]
    done = pl.pallas_call(
        functools.partial(begin_kernel, lat, lon, times),
        out_shape=shared,
        in_specs=[in_hbm] + [in_vmem] * (tiles - 2),
        out_specs=[in_vmem] * len(shared),
        scratch_shapes=[pltpu.SMEM(counts.shape, counts.dtype), pltpu.SemaphoreType.DMA],
        compiler_params=large,
        cost_estimate=pl.CostEstimate(
            flops=6 * begun * begun * HD,
            bytes_accessed=8 * begun * HD,
            transcendentals=begun * begun,
        ),
        name="begin",
    )(*from_hbm(counts), *there[: tiles - 2])
    made = pl.pallas_call(
        functools.partial(finish_kernel, lat, lon, times),
        out_shape=[block] * tiles,
        in_specs=[in_vmem] * (tiles + len(shared)),
        out_specs=[in_vmem] * tiles,
        scratch_shapes=[
            pltpu.VMEM((HD, wide), low),
            pltpu.VMEM((HD, wide), low),
            pltpu.VMEM((HD, wide), low),
            pltpu.VMEM((tiles - 1, wide, wide), f32),
            pltpu.VMEM((key_len, key_len), low),
            pltpu.VMEM((key_len, key_len), low),
        ],
        compiler_params=large,
        cost_estimate=pl.CostEstimate(
            flops=14 * key_len * key_len * HD - 6 * begun * begun * HD,
            bytes_accessed=16 * key_len * HD,
            transcendentals=key_len * key_len - begun * begun,
        ),
        name="finish",
    )(*there, *done)
    home = sent(in_steps(made), True)
    return tuple(
        pl.pallas_call(
            functools.partial(unpack_kernel, lat, lon, heads),
            out_shape=[whole] * 4,
            in_specs=[in_vmem] * tiles,
            out_specs=[in_hbm] * 4,
            scratch_shapes=[
                pltpu.VMEM((4, tile_len, width), low),
                pltpu.SemaphoreType.DMA((4, 4)),
            ],
            compiler_params=small,
            name="unpack",
        )(*home)
    )


def solution(mesh):
    tokens = P(("groups", "lat"), "lon", None, "head")

    def on_device(queries, *rest):
        lat, lon = mesh.shape["lat"], mesh.shape["lon"]
        one_tile = queries.shape[:2] == (1, 1)
        if one_tile and heads_fit(lat, lon, queries.shape[3] // HD):
            return by_heads(queries, *rest)
        return by_tiles(queries, *rest)

    return jax.shard_map(
        on_device,
        mesh=mesh,
        in_specs=(tokens,) * 4 + (P("groups", None),),
        out_specs=(tokens,) * 4,
        check_vma=False,
    )
```

```python
import functools
import math

import jax
import jax.numpy as jnp
from jax import lax
from jax.experimental import pallas as pl
from jax.experimental.pallas import tpu as pltpu
from jax.sharding import PartitionSpec as P

HD = 128


def with_halo(cells, sides, width, closed):
    for axis, dim in sides:
        count = lax.axis_size(axis)
        ends = count if closed else count - 1
        head = lax.slice_in_dim(cells, 0, width, axis=dim)
        tail = lax.slice_in_dim(cells, cells.shape[dim] - width, cells.shape[dim], axis=dim)
        cells = jnp.concatenate(
            [
                lax.ppermute(tail, axis, [(i, (i + 1) % count) for i in range(ends)]),
                cells,
                lax.ppermute(head, axis, [((i + 1) % count, i) for i in range(ends)]),
            ],
            axis=dim,
        )
    return cells


def passed_along(block, axis, distance):
    devices = range(lax.axis_size(axis))
    route = [((i - distance) % len(devices), i) for i in devices]
    return lax.ppermute(block, axis, route)


def neighbour_tiles(row_at, col_at, lat_tiles, lon_tiles):
    row_step = jnp.array([-1, -1, -1, 0, 0, 0, 1, 1, 1], dtype=jnp.int32)
    col_step = jnp.array([-1, 0, 1, -1, 0, 1, -1, 0, 1], dtype=jnp.int32)
    row_next = row_at + row_step
    across = (row_next < 0) | (row_next > lat_tiles - 1)
    col_next = (col_at + col_step + jnp.where(across, lon_tiles // 2, 0)) % lon_tiles
    row_next = jnp.clip(row_next, 0, lat_tiles - 1)
    return row_next * lon_tiles + col_next


def close_poles(rim_block, mirror):
    lat_index = lax.axis_index("lat")
    last_index = lax.axis_size("lat") - 1
    north_rim = jnp.where(lat_index == 0, mirror, rim_block[:1])
    south_rim = jnp.where(lat_index == last_index, mirror, rim_block[-1:])
    return jnp.concatenate([north_rim, rim_block[1:-1], south_rim], 0)


def around_pair(first_block, second_block):
    row_faces = (
        with_halo(first_block, (("lat", 0),), 1, False),
        with_halo(second_block, (("lat", 0),), 1, False),
    )
    mirror = passed_along((first_block, second_block), "lon", lax.axis_size("lon") // 2)
    column_a = close_poles(row_faces[0], mirror[0])
    column_b = close_poles(row_faces[1], mirror[1])
    return (
        with_halo(column_a, (("lon", 1),), 1, True),
        with_halo(column_b, (("lon", 1),), 1, True),
    )


def around_stats(log_total, out_dot):
    near_stats = (
        with_halo(log_total, (("lon", 1), ("lat", 0)), 1, True),
        with_halo(out_dot, (("lon", 1), ("lat", 0)), 1, True),
    )
    own_rows = log_total.shape[0]
    own_total = near_stats[0][1 : own_rows + 1]
    own_dot = near_stats[1][1 : own_rows + 1]
    mirror = passed_along((own_total, own_dot), "lon", lax.axis_size("lon") // 2)
    return (close_poles(near_stats[0], mirror[0]), close_poles(near_stats[1], mirror[1]))


def by_tiles(queries, key_tokens, value_tokens, out_grad, counts):
    own_rows = queries.shape[0]
    tile_len = queries.shape[2]
    feat_width = queries.shape[3]
    head_count = feat_width // HD
    lat_tiles = counts.shape[0]
    lon_tiles = counts.shape[1]
    row_base = lax.axis_index("lat") * own_rows
    col_at = lax.axis_index("lon")
    score_scale = 1.0 / math.sqrt(HD)
    positions = jnp.arange(tile_len, dtype=jnp.int32)
    flat_counts = counts.reshape(-1)
    near_k, near_v = around_pair(key_tokens, value_tokens)
    slot_ids = neighbour_tiles(row_base, col_at, lat_tiles, lon_tiles)
    key_valid = (positions[None, :] < flat_counts[slot_ids][:, None]).reshape(-1)
    near_keys = near_k.reshape(9 * tile_len, feat_width)
    near_values = near_v.reshape(9 * tile_len, feat_width)
    head_outs = []
    query_parts = []
    head_totals = []
    head_dots = []
    for head_index in range(head_count):
        columns = slice(head_index * HD, (head_index + 1) * HD)
        query_here = queries[0, 0, :, columns]
        grad_here = out_grad[0, 0, :, columns]
        keys_head = near_keys[:, columns]
        values_head = near_values[:, columns]
        scores = (
            jnp.einsum("qd,kd->qk", query_here, keys_head, preferred_element_type=jnp.float32)
            * score_scale
        )
        row_max = jnp.max(jnp.where(key_valid[None, :], scores, -1e30), axis=-1, keepdims=True)
        row_total = jnp.sum(
            jnp.where(key_valid[None, :], jnp.exp(scores - row_max), 0.0), axis=-1, keepdims=True
        )
        log_total = row_max + jnp.log(row_total)
        weights = jnp.where(key_valid[None, :], jnp.exp(scores - log_total), 0.0)
        weights_low = weights.astype(jnp.bfloat16)
        head_out = jnp.dot(weights_low, values_head, preferred_element_type=jnp.float32).astype(
            jnp.bfloat16
        )
        out_dot = jnp.sum(grad_here.astype(jnp.float32) * head_out.astype(jnp.float32), axis=-1)
        grad_weights = jnp.einsum(
            "qd,kd->qk", grad_here, values_head, preferred_element_type=jnp.float32
        )
        grad_scores = (weights * (grad_weights - out_dot[:, None])).astype(jnp.bfloat16)
        query_part = (
            jnp.dot(grad_scores, keys_head, preferred_element_type=jnp.float32) * score_scale
        )
        head_outs.append(head_out)
        query_parts.append(query_part.astype(jnp.bfloat16))
        head_totals.append(log_total[:, 0])
        head_dots.append(out_dot)
    attended = jnp.concatenate(head_outs, -1)[None, None]
    query_grad = jnp.concatenate(query_parts, -1)[None, None]
    own_totals = jnp.stack(head_totals)[None, None]
    own_dots = jnp.stack(head_dots)[None, None]
    near_q, near_g = around_pair(queries, out_grad)
    near_total, near_dot = around_stats(own_totals, own_dots)
    own_valid = positions < counts[row_base, col_at]
    near_queries = near_q.reshape(9 * tile_len, feat_width)
    near_grads = near_g.reshape(9 * tile_len, feat_width)
    key_parts = []
    value_parts = []
    for head_index in range(head_count):
        columns = slice(head_index * HD, (head_index + 1) * HD)
        queries_head = near_queries[:, columns]
        grads_head = near_grads[:, columns]
        keys_here = key_tokens[0, 0, :, columns]
        values_here = value_tokens[0, 0, :, columns]
        totals_head = near_total[:, :, head_index, :].reshape(9 * tile_len)
        dots_head = near_dot[:, :, head_index, :].reshape(9 * tile_len)
        scores = (
            jnp.einsum("qd,kd->qk", queries_head, keys_here, preferred_element_type=jnp.float32)
            * score_scale
        )
        weights = jnp.where(own_valid[None, :], jnp.exp(scores - totals_head[:, None]), 0.0)
        weights_low = weights.astype(jnp.bfloat16)
        value_part = jnp.einsum(
            "qk,qd->kd", weights_low, grads_head, preferred_element_type=jnp.float32
        )
        grad_weights = jnp.einsum(
            "qd,kd->qk", grads_head, values_here, preferred_element_type=jnp.float32
        )
        grad_scores = (weights * (grad_weights - dots_head[:, None])).astype(jnp.bfloat16)
        key_part = (
            jnp.einsum("qk,qd->kd", grad_scores, queries_head, preferred_element_type=jnp.float32)
            * score_scale
        )
        key_parts.append(key_part.astype(jnp.bfloat16))
        value_parts.append(value_part.astype(jnp.bfloat16))
    key_grad = jnp.concatenate(key_parts, -1)[None, None]
    value_grad = jnp.concatenate(value_parts, -1)[None, None]
    return (attended, query_grad, key_grad, value_grad)


def heads_fit(lat, lon, heads):
    fits = (
        heads % lat == 0
        and heads // lat <= lon <= 2 * (heads // lat)
        and lon % 2 == 0
        and 4 <= lat * lon <= 16
    )
    if not fits:
        return False
    first = relative_counts(lat, lon)
    return all(
        relative_counts(lat, lon, row, col, core) == first
        for row in range(lat)
        for col in range(lon)
        for core in range(2)
    )


def relative_counts(lat, lon, row=0, col=0, core=0):
    times = slot_counts(lat, lon)
    tile = []
    for step in steps_of(lat, lon, core):
        from_col = [c for c in range(lon) if column_after(c, step, lon) == col][0]
        tile.append((row - step[1]) % lat * lon + from_col)
    tile = in_slots(tile)
    return [[times[i][j] for j in tile] for i in tile]


def in_slots(found):
    return [*found[:-3], found[-1], *found[-3:-1]]


def in_steps(found):
    return [*found[:-3], *found[-2:], found[-3]]


def head_of(row, col, core, lat, lon, heads):
    per_row = heads // lat
    place = col - (1 - core % 2) * (lon - per_row)
    return row * per_row + place, (place >= 0) & (place < per_row)


def steps_of(lat, lon, core):
    half = lon // 2
    found = [(True, row_step, 0) for row_step in range(lat - 1, -1, -1)]
    for row_step in range(lat - 1, -1, -1):
        for col_step in range(1, half):
            turns = (True, row_step, col_step), (False, row_step, col_step)
            found.extend(turns[::-1] if core % 2 else turns)
    found.extend((False, row_step, 0) for row_step in range(1, lat))
    return found + [(False, 0, 0)]


def column_after(col, step, lon):
    half = lon // 2
    other = col // half ^ int(step[0])
    return other * half + (col + step[2]) % half


def partner(row, col, core, n, lat, lon, back=False):
    places = []
    for which in (0, 1):
        step = steps_of(lat, lon, which)[n]
        to_row = lax.rem(row + (lat - step[1] if back else step[1]), lat)
        to_col = jnp.int32(0)
        for here in range(lon):
            there = column_after(here, step, lon)
            if back:
                to_col = jnp.where(col == there, here, to_col)
            else:
                to_col = jnp.where(col == here, there, to_col)
        places.append((to_row, to_col))
    return [jnp.where(core % 2 == 0, a, b) for a, b in zip(*places)]


def routes(n, lat, lon, cores, heads, back):
    pairs = []
    for row in range(lat):
        for col in range(lon):
            for core in range(cores):
                step = steps_of(lat, lon, core)[n]
                to_row, to_col = (row + step[1]) % lat, column_after(col, step, lon)
                if head_of(to_row, to_col, core, lat, lon, heads)[1]:
                    here = (col * lat + row) * cores + core
                    there = (to_col * lat + to_row) * cores + core
                    pairs.append((there, here) if back else (here, there))
    return pairs


def slot_counts(lat, lon):
    times = [[0] * (lat * lon) for _ in range(lat * lon)]
    for row in range(lat):
        for col in range(lon):
            for a in (-1, 0, 1):
                for b in (-1, 0, 1):
                    near_row, near_col = row + a, col + b
                    if near_row < 0 or near_row > lat - 1:
                        near_col += lon // 2
                        near_row = min(max(near_row, 0), lat - 1)
                    times[row * lon + col][near_row * lon + near_col % lon] += 1
    return times


def pack_kernel(lat, lon, heads, *refs):
    tensors, blocks, whole, sems = refs[:4], refs[4:-2], refs[-2], refs[-1]
    row, col, core = (lax.axis_index(a) for a in ("lat", "lon", "head"))
    parts = sems.shape[1]
    size = whole.shape[1] // parts
    copies = []
    for n in range(parts):
        rows = pl.ds(n * size, size)
        for t, tensor in enumerate(tensors):
            copies.append(
                pltpu.make_async_copy(
                    tensor.at[0, 0, rows, :], whole.at[t, rows, :], sems.at[t, n]
                )
            )
    for copy in copies:
        copy.start()
    for n in range(parts):
        rows = slice(n * size, (n + 1) * size)
        for copy in copies[4 * n : 4 * n + 4]:
            copy.wait()
        for m, block in enumerate(blocks):
            head, used = head_of(*partner(row, col, core, m, lat, lon), core, lat, lon, heads)

            @pl.when(used)
            def _():
                features = pl.ds(pl.multiple_of(head * HD, HD), HD)
                for t in range(4):
                    block[t, rows, :] = whole[t, rows, features]


def unpack_kernel(lat, lon, heads, *refs):
    blocks, tensors, whole, sems = refs[:-6], refs[-6:-2], refs[-2], refs[-1]
    row, col, core = (lax.axis_index(a) for a in ("lat", "lon", "head"))
    parts = sems.shape[1]
    size = whole.shape[1] // parts
    copies = []
    for n in range(parts):
        rows = slice(n * size, (n + 1) * size)
        for m, block in enumerate(blocks):
            head, used = head_of(*partner(row, col, core, m, lat, lon), core, lat, lon, heads)

            @pl.when(used)
            def _():
                features = pl.ds(pl.multiple_of(head * HD, HD), HD)
                for t in range(4):
                    whole[t, rows, features] = block[t, rows, :]

        rows = pl.ds(n * size, size)
        for t, tensor in enumerate(tensors):
            copies.append(
                pltpu.make_async_copy(
                    whole.at[t, rows, :], tensor.at[0, 0, rows, :], sems.at[t, n]
                )
            )
            copies[-1].start()
    for copy in copies:
        copy.wait()


class Sphere:
    def __init__(self, lat, lon, times, key_marks, query_marks):
        self.tiles = lat * lon
        self.times = times
        self.key_marks, self.query_marks = key_marks, query_marks
        self.size = key_marks.shape[1]
        self.wide = 2 * self.size
        self.rounds = self.tiles // 2
        self.scale = 1.0 / math.sqrt(HD)
        self.of_tile = lax.broadcasted_iota(jnp.int32, (1, self.wide), 1) // self.size
        self.held = [None] * self.tiles

    def mark(self, limits):
        shape = (self.size, HD)
        key_row = lax.broadcasted_iota(jnp.int32, shape, 0)
        lane = lax.broadcasted_iota(jnp.int32, shape, 1)
        for j in range(self.tiles):
            unseen = (lane == 0) & (key_row >= limits[j])
            key_mark = jnp.where(unseen, -1e30, jnp.where(lane == j + 1, 1.0, 0.0))
            self.key_marks[j] = key_mark.astype(self.key_marks.dtype)
            apart = jnp.zeros(shape, jnp.bool_)
            for k in range(self.tiles):
                if self.times[j][k] == 0:
                    apart = apart | (lane == k + 1)
            query_mark = jnp.where(apart, -1e30, jnp.where(lane == 0, 1.0, 0.0))
            self.query_marks[j] = query_mark.astype(self.query_marks.dtype)

    def rows(self, j):
        return slice(j * self.size, (j + 1) * self.size)

    def lanes(self, t):
        return slice(t * self.wide, (t + 1) * self.wide)

    def stacked(self, t, n):
        return jnp.concatenate([self.held[2 * t + k][n] for k in range(2)], 0)

    def marked(self, t, n, marks):
        parts = [(self.held[i][n], marks[i]) for i in (2 * t, 2 * t + 1)]
        return jnp.concatenate([jnp.concatenate(part, 1) for part in parts], 0)

    def score(self, t, u):
        return contract_last(
            self.marked(u, 1, self.key_marks), self.marked(t, 0, self.query_marks)
        )

    def grad_weight(self, t, u):
        return contract_last(self.stacked(u, 2), self.stacked(t, 3))

    def exponential(self, scores, top):
        return jnp.exp2((scores - top) * (self.scale * math.log2(math.e)))

    def named(self, t, j):
        line = jnp.ones((1, self.wide), jnp.float32)
        for k in range(2):
            if self.times[2 * t + k][j] > 1:
                line = jnp.where(self.of_tile == k, float(self.times[2 * t + k][j]), line)
        return line

    def folded(self, part, op):
        return op(part.reshape(part.shape[0] // 8, 8, self.wide), axis=0)

    def added(self, total, t, u, parts):
        for k in range(2):
            part = self.folded(parts[self.rows(k), :], jnp.sum) * self.named(t, 2 * u + k)
            total = part if total is None else total + part
        return total


def contract_last(a, b):
    return lax.dot_general(a, b, (((1,), (1,)), ((), ())), preferred_element_type=jnp.float32)


def greater(a, b):
    return b if a is None else jnp.maximum(a, b)


def begin_kernel(lat, lon, times, *refs):
    tiles = lat * lon
    all_counts, blocks, outs = refs[0], refs[1 : tiles - 1], refs[tiles - 1 :]
    key_marks, query_marks, keys_t, values_t, grads_t, scores, grad_weights, stats = outs[:8]
    counts, sem = outs[8:]
    sphere = Sphere(lat, lon, times, key_marks, query_marks)
    sphere.held[: tiles - 2] = blocks
    rounds = sphere.rounds - 1
    copy = pltpu.make_async_copy(all_counts, counts, sem)
    copy.start()
    for t in range(rounds):
        for u in range(rounds):
            grad_weights[t, sphere.lanes(u), :] = sphere.grad_weight(t, u)
        for i in (2 * t, 2 * t + 1):
            keys_t[:, sphere.rows(i)] = blocks[i][1].T
            values_t[:, sphere.rows(i)] = blocks[i][2].T
            grads_t[:, sphere.rows(i)] = blocks[i][3].T
    copy.wait()
    row, col, core = (lax.axis_index(a) for a in ("lat", "lon", "head"))
    limits = [
        counts[tuple(partner(row, col, core, n, lat, lon, True))] for n in range(tiles)
    ]
    sphere.mark(in_slots(limits))
    best, total = [None] * rounds, [None] * rounds

    def score(t, u):
        part = sphere.score(t, u)
        scores[t, sphere.lanes(u), :] = part
        best[t] = greater(best[t], sphere.folded(part, jnp.max))

    for u in range(rounds):
        score(0, u)
    for t in range(rounds):
        best[t] = jnp.max(best[t], axis=0, keepdims=True)
        for u in range(rounds):
            part = sphere.exponential(scores[t, sphere.lanes(u), :], best[t])
            scores[t, sphere.lanes(u), :] = part
            total[t] = sphere.added(total[t], t, u, part)
            if t + 1 < rounds:
                score(t + 1, u)
        stats[t, :8, :] = jnp.broadcast_to(best[t], (8, sphere.wide))
        stats[t, 8:, :] = total[t]


def finish_kernel(lat, lon, times, *refs):
    tiles = lat * lon
    blocks, refs = refs[:tiles], refs[tiles:]
    key_marks, query_marks, keys_t, values_t, grads_t, scores, grad_weights, stats = refs[:8]
    made, refs = refs[8 : 8 + tiles], refs[8 + tiles :]
    last_keys_t, last_values_t, last_grads_t, more_scores, weights_low, grads_low = refs
    sphere = Sphere(lat, lon, times, key_marks, query_marks)
    sphere.held[:] = blocks
    f32, low = jnp.float32, weights_low.dtype
    rounds, last = sphere.rounds, sphere.rounds - 1
    best, total, old, share, out_dot = ([None] * rounds for _ in range(5))
    early = slice(0, last * sphere.wide)
    late = sphere.lanes(last)

    def held_scores(t, j):
        if t < last and j // 2 < last:
            return scores.at[t, sphere.rows(j), :]
        if t < last:
            return more_scores.at[t, sphere.rows(j - 2 * last), :]
        return more_scores.at[last + j // 2, sphere.rows(j % 2), :]

    def score(t, u):
        part = sphere.score(t, u)
        for k in range(2):
            held_scores(t, 2 * u + k)[...] = part[sphere.rows(k), :]
        best[t] = greater(best[t], sphere.folded(part, jnp.max))

    def exponential(t, u):
        parts = []
        for j in (2 * u, 2 * u + 1):
            parts.append(sphere.exponential(held_scores(t, j)[...], best[t]))
            held_scores(t, j)[...] = parts[-1]
        total[t] = sphere.added(total[t], t, u, jnp.concatenate(parts, 0))

    def settle(t):
        before = stats[t, :1, :]
        best[t] = jnp.maximum(before, jnp.max(best[t], axis=0, keepdims=True))
        old[t] = sphere.exponential(before, best[t])
        total[t] = stats[t, 8:, :] * old[t]
        exponential(t, last)
        share[t] = 1.0 / jnp.sum(total[t], axis=0, keepdims=True)

    def factor(t, j):
        line = share[t] * sphere.named(t, j)
        return line * old[t] if t < last and j // 2 < last else line

    def weight(t, u):
        for j in (2 * u, 2 * u + 1):
            part = held_scores(t, j)[...] * factor(t, j)
            weights_low[sphere.rows(j), sphere.lanes(t)] = part.astype(low)

    def from_keys(first_t, last_t, low_scores, t):
        lanes = sphere.lanes(t)
        return jnp.dot(
            first_t[...], low_scores[early, lanes], preferred_element_type=f32
        ) + jnp.dot(last_t[...], low_scores[late, lanes], preferred_element_type=f32)

    def attend(t):
        out_t = from_keys(values_t, last_values_t, weights_low, t).astype(low)
        grad_t = grads_t[:, sphere.lanes(t)] if t < last else last_grads_t[...]
        out_dot[t] = jnp.sum(grad_t.astype(f32) * out_t.astype(f32), axis=0, keepdims=True)
        for k in range(2):
            made[2 * t + k][0] = out_t[:, sphere.rows(k)].T

    def grad_score(t, u):
        if t < last and u < last:
            part = grad_weights[t, sphere.lanes(u), :]
        else:
            part = sphere.grad_weight(t, u)
        for k in range(2):
            j = 2 * u + k
            weights = held_scores(t, j)[...] * factor(t, j)
            grad = weights * (part[sphere.rows(k), :] - out_dot[t])
            grads_low[sphere.rows(j), sphere.lanes(t)] = grad.astype(low)

    def query_grad(t):
        query_t = (from_keys(keys_t, last_keys_t, grads_low, t) * sphere.scale).astype(low)
        for k in range(2):
            made[2 * t + k][1] = query_t[:, sphere.rows(k)].T

    def key_side(n, low_scores, to, factor):
        part = jnp.dot(
            low_scores[...],
            jnp.concatenate([block[n] for block in blocks], 0),
            preferred_element_type=f32,
        )
        for j in range(tiles):
            made[j][to] = (part[sphere.rows(j), :] * factor).astype(low)

    for t in range(last):
        score(t, last)
    for k in range(2):
        block = blocks[2 * last + k]
        last_keys_t[:, sphere.rows(k)] = block[1].T
        last_values_t[:, sphere.rows(k)] = block[2].T
        last_grads_t[:, sphere.rows(k)] = block[3].T
    for t in range(last):
        settle(t)
        if t > 0:
            attend(t - 1)
        if t > 1:
            query_grad(t - 2)
        for u in range(rounds):
            weight(t, u)
            if t == 0:
                score(last, u)
            if t == 1 or last == 1:
                if u == 0:
                    best[last] = jnp.max(best[last], axis=0, keepdims=True)
                exponential(last, u)
            if t > 0:
                grad_score(t - 1, u)
    share[last] = 1.0 / jnp.sum(total[last], axis=0, keepdims=True)
    attend(last - 1)
    if last > 1:
        query_grad(last - 2)
    for u in range(rounds):
        weight(last, u)
        grad_score(last - 1, u)
    attend(last)
    key_side(3, weights_low, 3, 1.0)
    query_grad(last - 1)
    for u in range(rounds):
        grad_score(last, u)
    query_grad(last)
    key_side(0, grads_low, 2, sphere.scale)


def by_heads(queries, key_tokens, value_tokens, out_grad, counts):
    lat, lon, cores = (lax.axis_size(a) for a in ("lat", "lon", "head"))
    tiles = lat * lon
    tile_len, width = queries.shape[2], queries.shape[3]
    heads = width // HD
    low, f32 = queries.dtype, jnp.float32
    in_vmem = pl.BlockSpec(memory_space=pltpu.VMEM)
    in_hbm = pl.BlockSpec(memory_space=pltpu.HBM)
    whole = jax.ShapeDtypeStruct(queries.shape, low)
    block = pltpu.VMEM((4, tile_len, HD), low)
    small = pltpu.CompilerParams(vmem_limit_bytes=6 * 1024 * 1024)

    def sent(blocks, back):
        axes = ("lon", "lat", "head")
        moves = list(range(tiles - 1))
        if back:
            full, mixed, along = moves[:lat], moves[lat : 1 - lat], moves[1 - lat :]
            moves = full + mixed[::2] + mixed[1::2] + along
        found = list(blocks)
        for n in moves:
            found[n] = lax.ppermute(found[n], axes, routes(n, lat, lon, cores, heads, back))
        return found

    def from_hbm(*arrays):
        return [pltpu.with_memory_space_constraint(x, pltpu.HBM) for x in arrays]

    packed = pl.pallas_call(
        functools.partial(pack_kernel, lat, lon, heads),
        out_shape=[block] * tiles,
        in_specs=[in_hbm] * 4,
        out_specs=[in_vmem] * tiles,
        scratch_shapes=[
            pltpu.VMEM((4, tile_len, width), low),
            pltpu.SemaphoreType.DMA((4, 4)),
        ],
        compiler_params=small,
        name="pack",
    )(*from_hbm(queries, key_tokens, value_tokens, out_grad))
    there = in_slots(sent(packed, False))
    key_len, wide, begun = tiles * tile_len, 2 * tile_len, (tiles - 2) * tile_len
    times = relative_counts(lat, lon)
    large = pltpu.CompilerParams(vmem_limit_bytes=24 * 1024 * 1024)
    shared = [
        pltpu.VMEM((tiles, tile_len, HD), low),
        pltpu.VMEM((tiles, tile_len, HD), low),
        pltpu.VMEM((HD, begun), low),
        pltpu.VMEM((HD, begun), low),
        pltpu.VMEM((HD, begun), low),
        pltpu.VMEM((tiles // 2 - 1, begun, wide), f32),
        pltpu.VMEM((tiles // 2 - 1, begun, wide), f32),
        pltpu.VMEM((tiles // 2 - 1, 16, wide), f32),
    ]
    done = pl.pallas_call(
        functools.partial(begin_kernel, lat, lon, times),
        out_shape=shared,
        in_specs=[in_hbm] + [in_vmem] * (tiles - 2),
        out_specs=[in_vmem] * len(shared),
        scratch_shapes=[pltpu.SMEM(counts.shape, counts.dtype), pltpu.SemaphoreType.DMA],
        compiler_params=large,
        cost_estimate=pl.CostEstimate(
            flops=6 * begun * begun * HD,
            bytes_accessed=8 * begun * HD,
            transcendentals=begun * begun,
        ),
        name="begin",
    )(*from_hbm(counts), *there[: tiles - 2])
    made = pl.pallas_call(
        functools.partial(finish_kernel, lat, lon, times),
        out_shape=[block] * tiles,
        in_specs=[in_vmem] * (tiles + len(shared)),
        out_specs=[in_vmem] * tiles,
        scratch_shapes=[
            pltpu.VMEM((HD, wide), low),
            pltpu.VMEM((HD, wide), low),
            pltpu.VMEM((HD, wide), low),
            pltpu.VMEM((tiles - 1, wide, wide), f32),
            pltpu.VMEM((key_len, key_len), low),
            pltpu.VMEM((key_len, key_len), low),
        ],
        compiler_params=large,
        cost_estimate=pl.CostEstimate(
            flops=14 * key_len * key_len * HD - 6 * begun * begun * HD,
            bytes_accessed=16 * key_len * HD,
            transcendentals=key_len * key_len - begun * begun,
        ),
        name="finish",
    )(*there, *done)
    home = sent(in_steps(made), True)
    return tuple(
        pl.pallas_call(
            functools.partial(unpack_kernel, lat, lon, heads),
            out_shape=[whole] * 4,
            in_specs=[in_vmem] * tiles,
            out_specs=[in_hbm] * 4,
            scratch_shapes=[
                pltpu.VMEM((4, tile_len, width), low),
                pltpu.SemaphoreType.DMA((4, 4)),
            ],
            compiler_params=small,
            name="unpack",
        )(*home)
    )


def solution(mesh):
    tokens = P(("groups", "lat"), "lon", None, "head")

    def on_device(queries, *rest):
        lat, lon = mesh.shape["lat"], mesh.shape["lon"]
        one_tile = queries.shape[:2] == (1, 1)
        if one_tile and heads_fit(lat, lon, queries.shape[3] // HD):
            return by_heads(queries, *rest)
        return by_tiles(queries, *rest)

    return jax.shard_map(
        on_device,
        mesh=mesh,
        in_specs=(tokens,) * 4 + (P("groups", None),),
        out_specs=(tokens,) * 4,
        check_vma=False,
    )
```

```python
import functools
import math

import jax
import jax.numpy as jnp
from jax import lax
from jax.experimental import pallas as pl
from jax.experimental.pallas import tpu as pltpu
from jax.sharding import PartitionSpec as P

HD = 128


def with_halo(cells, sides, width, closed):
    for axis, dim in sides:
        count = lax.axis_size(axis)
        ends = count if closed else count - 1
        head = lax.slice_in_dim(cells, 0, width, axis=dim)
        tail = lax.slice_in_dim(cells, cells.shape[dim] - width, cells.shape[dim], axis=dim)
        cells = jnp.concatenate(
            [
                lax.ppermute(tail, axis, [(i, (i + 1) % count) for i in range(ends)]),
                cells,
                lax.ppermute(head, axis, [((i + 1) % count, i) for i in range(ends)]),
            ],
            axis=dim,
        )
    return cells


def passed_along(block, axis, distance):
    devices = range(lax.axis_size(axis))
    route = [((i - distance) % len(devices), i) for i in devices]
    return lax.ppermute(block, axis, route)


def neighbour_tiles(row_at, col_at, lat_tiles, lon_tiles):
    row_step = jnp.array([-1, -1, -1, 0, 0, 0, 1, 1, 1], dtype=jnp.int32)
    col_step = jnp.array([-1, 0, 1, -1, 0, 1, -1, 0, 1], dtype=jnp.int32)
    row_next = row_at + row_step
    across = (row_next < 0) | (row_next > lat_tiles - 1)
    col_next = (col_at + col_step + jnp.where(across, lon_tiles // 2, 0)) % lon_tiles
    row_next = jnp.clip(row_next, 0, lat_tiles - 1)
    return row_next * lon_tiles + col_next


def close_poles(rim_block, mirror):
    lat_index = lax.axis_index("lat")
    last_index = lax.axis_size("lat") - 1
    north_rim = jnp.where(lat_index == 0, mirror, rim_block[:1])
    south_rim = jnp.where(lat_index == last_index, mirror, rim_block[-1:])
    return jnp.concatenate([north_rim, rim_block[1:-1], south_rim], 0)


def around_pair(first_block, second_block):
    row_faces = (
        with_halo(first_block, (("lat", 0),), 1, False),
        with_halo(second_block, (("lat", 0),), 1, False),
    )
    mirror = passed_along((first_block, second_block), "lon", lax.axis_size("lon") // 2)
    column_a = close_poles(row_faces[0], mirror[0])
    column_b = close_poles(row_faces[1], mirror[1])
    return (
        with_halo(column_a, (("lon", 1),), 1, True),
        with_halo(column_b, (("lon", 1),), 1, True),
    )


def around_stats(log_total, out_dot):
    near_stats = (
        with_halo(log_total, (("lon", 1), ("lat", 0)), 1, True),
        with_halo(out_dot, (("lon", 1), ("lat", 0)), 1, True),
    )
    own_rows = log_total.shape[0]
    own_total = near_stats[0][1 : own_rows + 1]
    own_dot = near_stats[1][1 : own_rows + 1]
    mirror = passed_along((own_total, own_dot), "lon", lax.axis_size("lon") // 2)
    return (close_poles(near_stats[0], mirror[0]), close_poles(near_stats[1], mirror[1]))


def by_tiles(queries, key_tokens, value_tokens, out_grad, counts):
    own_rows = queries.shape[0]
    tile_len = queries.shape[2]
    feat_width = queries.shape[3]
    head_count = feat_width // HD
    lat_tiles = counts.shape[0]
    lon_tiles = counts.shape[1]
    row_base = lax.axis_index("lat") * own_rows
    col_at = lax.axis_index("lon")
    score_scale = 1.0 / math.sqrt(HD)
    positions = jnp.arange(tile_len, dtype=jnp.int32)
    flat_counts = counts.reshape(-1)
    near_k, near_v = around_pair(key_tokens, value_tokens)
    slot_ids = neighbour_tiles(row_base, col_at, lat_tiles, lon_tiles)
    key_valid = (positions[None, :] < flat_counts[slot_ids][:, None]).reshape(-1)
    near_keys = near_k.reshape(9 * tile_len, feat_width)
    near_values = near_v.reshape(9 * tile_len, feat_width)
    head_outs = []
    query_parts = []
    head_totals = []
    head_dots = []
    for head_index in range(head_count):
        columns = slice(head_index * HD, (head_index + 1) * HD)
        query_here = queries[0, 0, :, columns]
        grad_here = out_grad[0, 0, :, columns]
        keys_head = near_keys[:, columns]
        values_head = near_values[:, columns]
        scores = (
            jnp.einsum("qd,kd->qk", query_here, keys_head, preferred_element_type=jnp.float32)
            * score_scale
        )
        row_max = jnp.max(jnp.where(key_valid[None, :], scores, -1e30), axis=-1, keepdims=True)
        row_total = jnp.sum(
            jnp.where(key_valid[None, :], jnp.exp(scores - row_max), 0.0), axis=-1, keepdims=True
        )
        log_total = row_max + jnp.log(row_total)
        weights = jnp.where(key_valid[None, :], jnp.exp(scores - log_total), 0.0)
        weights_low = weights.astype(jnp.bfloat16)
        head_out = jnp.dot(weights_low, values_head, preferred_element_type=jnp.float32).astype(
            jnp.bfloat16
        )
        out_dot = jnp.sum(grad_here.astype(jnp.float32) * head_out.astype(jnp.float32), axis=-1)
        grad_weights = jnp.einsum(
            "qd,kd->qk", grad_here, values_head, preferred_element_type=jnp.float32
        )
        grad_scores = (weights * (grad_weights - out_dot[:, None])).astype(jnp.bfloat16)
        query_part = (
            jnp.dot(grad_scores, keys_head, preferred_element_type=jnp.float32) * score_scale
        )
        head_outs.append(head_out)
        query_parts.append(query_part.astype(jnp.bfloat16))
        head_totals.append(log_total[:, 0])
        head_dots.append(out_dot)
    attended = jnp.concatenate(head_outs, -1)[None, None]
    query_grad = jnp.concatenate(query_parts, -1)[None, None]
    own_totals = jnp.stack(head_totals)[None, None]
    own_dots = jnp.stack(head_dots)[None, None]
    near_q, near_g = around_pair(queries, out_grad)
    near_total, near_dot = around_stats(own_totals, own_dots)
    own_valid = positions < counts[row_base, col_at]
    near_queries = near_q.reshape(9 * tile_len, feat_width)
    near_grads = near_g.reshape(9 * tile_len, feat_width)
    key_parts = []
    value_parts = []
    for head_index in range(head_count):
        columns = slice(head_index * HD, (head_index + 1) * HD)
        queries_head = near_queries[:, columns]
        grads_head = near_grads[:, columns]
        keys_here = key_tokens[0, 0, :, columns]
        values_here = value_tokens[0, 0, :, columns]
        totals_head = near_total[:, :, head_index, :].reshape(9 * tile_len)
        dots_head = near_dot[:, :, head_index, :].reshape(9 * tile_len)
        scores = (
            jnp.einsum("qd,kd->qk", queries_head, keys_here, preferred_element_type=jnp.float32)
            * score_scale
        )
        weights = jnp.where(own_valid[None, :], jnp.exp(scores - totals_head[:, None]), 0.0)
        weights_low = weights.astype(jnp.bfloat16)
        value_part = jnp.einsum(
            "qk,qd->kd", weights_low, grads_head, preferred_element_type=jnp.float32
        )
        grad_weights = jnp.einsum(
            "qd,kd->qk", grads_head, values_here, preferred_element_type=jnp.float32
        )
        grad_scores = (weights * (grad_weights - dots_head[:, None])).astype(jnp.bfloat16)
        key_part = (
            jnp.einsum("qk,qd->kd", grad_scores, queries_head, preferred_element_type=jnp.float32)
            * score_scale
        )
        key_parts.append(key_part.astype(jnp.bfloat16))
        value_parts.append(value_part.astype(jnp.bfloat16))
    key_grad = jnp.concatenate(key_parts, -1)[None, None]
    value_grad = jnp.concatenate(value_parts, -1)[None, None]
    return (attended, query_grad, key_grad, value_grad)


def heads_fit(lat, lon, heads):
    fits = (
        heads % lat == 0
        and heads // lat <= lon <= 2 * (heads // lat)
        and lon % 2 == 0
        and 4 <= lat * lon <= 16
    )
    if not fits:
        return False
    first = relative_counts(lat, lon)
    return all(
        relative_counts(lat, lon, row, col, core) == first
        for row in range(lat)
        for col in range(lon)
        for core in range(2)
    )


def relative_counts(lat, lon, row=0, col=0, core=0):
    times = slot_counts(lat, lon)
    tile = []
    for step in steps_of(lat, lon, core):
        from_col = [c for c in range(lon) if column_after(c, step, lon) == col][0]
        tile.append((row - step[1]) % lat * lon + from_col)
    tile = in_slots(tile)
    return [[times[i][j] for j in tile] for i in tile]


def in_slots(found):
    return [*found[:-3], found[-1], *found[-3:-1]]


def in_steps(found):
    return [*found[:-3], *found[-2:], found[-3]]


def head_of(row, col, core, lat, lon, heads):
    per_row = heads // lat
    place = col - (1 - core % 2) * (lon - per_row)
    return row * per_row + place, (place >= 0) & (place < per_row)


def steps_of(lat, lon, core):
    half = lon // 2
    found = [(True, row_step, 0) for row_step in range(lat - 1, -1, -1)]
    for row_step in range(lat - 1, -1, -1):
        for col_step in range(1, half):
            turns = (True, row_step, col_step), (False, row_step, col_step)
            found.extend(turns[::-1] if core % 2 else turns)
    found.extend((False, row_step, 0) for row_step in range(1, lat))
    return found + [(False, 0, 0)]


def column_after(col, step, lon):
    half = lon // 2
    other = col // half ^ int(step[0])
    return other * half + (col + step[2]) % half


def partner(row, col, core, n, lat, lon, back=False):
    places = []
    for which in (0, 1):
        step = steps_of(lat, lon, which)[n]
        to_row = lax.rem(row + (lat - step[1] if back else step[1]), lat)
        to_col = jnp.int32(0)
        for here in range(lon):
            there = column_after(here, step, lon)
            if back:
                to_col = jnp.where(col == there, here, to_col)
            else:
                to_col = jnp.where(col == here, there, to_col)
        places.append((to_row, to_col))
    return [jnp.where(core % 2 == 0, a, b) for a, b in zip(*places)]


def routes(n, lat, lon, cores, heads, back):
    pairs = []
    for row in range(lat):
        for col in range(lon):
            for core in range(cores):
                step = steps_of(lat, lon, core)[n]
                to_row, to_col = (row + step[1]) % lat, column_after(col, step, lon)
                if head_of(to_row, to_col, core, lat, lon, heads)[1]:
                    here = (col * lat + row) * cores + core
                    there = (to_col * lat + to_row) * cores + core
                    pairs.append((there, here) if back else (here, there))
    return pairs


def slot_counts(lat, lon):
    times = [[0] * (lat * lon) for _ in range(lat * lon)]
    for row in range(lat):
        for col in range(lon):
            for a in (-1, 0, 1):
                for b in (-1, 0, 1):
                    near_row, near_col = row + a, col + b
                    if near_row < 0 or near_row > lat - 1:
                        near_col += lon // 2
                        near_row = min(max(near_row, 0), lat - 1)
                    times[row * lon + col][near_row * lon + near_col % lon] += 1
    return times


def pack_kernel(lat, lon, heads, *refs):
    tensors, blocks, whole, sems = refs[:4], refs[4:-2], refs[-2], refs[-1]
    row, col, core = (lax.axis_index(a) for a in ("lat", "lon", "head"))
    parts = sems.shape[1]
    size = whole.shape[1] // parts
    copies = []
    for n in range(parts):
        rows = pl.ds(n * size, size)
        for t, tensor in enumerate(tensors):
            copies.append(
                pltpu.make_async_copy(
                    tensor.at[0, 0, rows, :], whole.at[t, rows, :], sems.at[t, n]
                )
            )
    for copy in copies:
        copy.start()
    for n in range(parts):
        rows = slice(n * size, (n + 1) * size)
        for copy in copies[4 * n : 4 * n + 4]:
            copy.wait()
        for m, block in enumerate(blocks):
            head, used = head_of(*partner(row, col, core, m, lat, lon), core, lat, lon, heads)

            @pl.when(used)
            def _():
                features = pl.ds(pl.multiple_of(head * HD, HD), HD)
                for t in range(4):
                    block[t, rows, :] = whole[t, rows, features]


def unpack_kernel(lat, lon, heads, *refs):
    blocks, tensors, whole, sems = refs[:-6], refs[-6:-2], refs[-2], refs[-1]
    row, col, core = (lax.axis_index(a) for a in ("lat", "lon", "head"))
    parts = sems.shape[1]
    size = whole.shape[1] // parts
    copies = []
    for n in range(parts):
        rows = slice(n * size, (n + 1) * size)
        for m, block in enumerate(blocks):
            head, used = head_of(*partner(row, col, core, m, lat, lon), core, lat, lon, heads)

            @pl.when(used)
            def _():
                features = pl.ds(pl.multiple_of(head * HD, HD), HD)
                for t in range(4):
                    whole[t, rows, features] = block[t, rows, :]

        rows = pl.ds(n * size, size)
        for t, tensor in enumerate(tensors):
            copies.append(
                pltpu.make_async_copy(
                    whole.at[t, rows, :], tensor.at[0, 0, rows, :], sems.at[t, n]
                )
            )
            copies[-1].start()
    for copy in copies:
        copy.wait()


class Sphere:
    def __init__(self, lat, lon, times, key_marks, query_marks):
        self.tiles = lat * lon
        self.times = times
        self.key_marks, self.query_marks = key_marks, query_marks
        self.size = key_marks.shape[1]
        self.wide = 2 * self.size
        self.rounds = self.tiles // 2
        self.scale = 1.0 / math.sqrt(HD)
        self.of_tile = lax.broadcasted_iota(jnp.int32, (1, self.wide), 1) // self.size
        self.held = [None] * self.tiles

    def mark(self, limits):
        shape = (self.size, HD)
        key_row = lax.broadcasted_iota(jnp.int32, shape, 0)
        lane = lax.broadcasted_iota(jnp.int32, shape, 1)
        for j in range(self.tiles):
            unseen = (lane == 0) & (key_row >= limits[j])
            key_mark = jnp.where(unseen, -1e30, jnp.where(lane == j + 1, 1.0, 0.0))
            self.key_marks[j] = key_mark.astype(self.key_marks.dtype)
            apart = jnp.zeros(shape, jnp.bool_)
            for k in range(self.tiles):
                if self.times[j][k] == 0:
                    apart = apart | (lane == k + 1)
            query_mark = jnp.where(apart, -1e30, jnp.where(lane == 0, 1.0, 0.0))
            self.query_marks[j] = query_mark.astype(self.query_marks.dtype)

    def rows(self, j):
        return slice(j * self.size, (j + 1) * self.size)

    def lanes(self, t):
        return slice(t * self.wide, (t + 1) * self.wide)

    def stacked(self, t, n):
        return jnp.concatenate([self.held[2 * t + k][n] for k in range(2)], 0)

    def marked(self, t, n, marks):
        parts = [(self.held[i][n], marks[i]) for i in (2 * t, 2 * t + 1)]
        return jnp.concatenate([jnp.concatenate(part, 1) for part in parts], 0)

    def score(self, t, u):
        return contract_last(
            self.marked(u, 1, self.key_marks), self.marked(t, 0, self.query_marks)
        )

    def grad_weight(self, t, u):
        return contract_last(self.stacked(u, 2), self.stacked(t, 3))

    def exponential(self, scores, top):
        return jnp.exp2((scores - top) * (self.scale * math.log2(math.e)))

    def named(self, t, j):
        line = jnp.ones((1, self.wide), jnp.float32)
        for k in range(2):
            if self.times[2 * t + k][j] > 1:
                line = jnp.where(self.of_tile == k, float(self.times[2 * t + k][j]), line)
        return line

    def folded(self, part, op):
        return op(part.reshape(part.shape[0] // 8, 8, self.wide), axis=0)

    def added(self, total, t, u, parts):
        for k in range(2):
            part = self.folded(parts[self.rows(k), :], jnp.sum) * self.named(t, 2 * u + k)
            total = part if total is None else total + part
        return total


def contract_last(a, b):
    return lax.dot_general(a, b, (((1,), (1,)), ((), ())), preferred_element_type=jnp.float32)


def greater(a, b):
    return b if a is None else jnp.maximum(a, b)


def begin_kernel(lat, lon, times, *refs):
    tiles = lat * lon
    all_counts, blocks, outs = refs[0], refs[1 : tiles - 1], refs[tiles - 1 :]
    key_marks, query_marks, keys_t, values_t, grads_t, scores, grad_weights, stats = outs[:8]
    counts, sem = outs[8:]
    sphere = Sphere(lat, lon, times, key_marks, query_marks)
    sphere.held[: tiles - 2] = blocks
    rounds = sphere.rounds - 1
    copy = pltpu.make_async_copy(all_counts, counts, sem)
    copy.start()
    for t in range(rounds):
        for u in range(rounds):
            grad_weights[t, sphere.lanes(u), :] = sphere.grad_weight(t, u)
        for i in (2 * t, 2 * t + 1):
            keys_t[:, sphere.rows(i)] = blocks[i][1].T
            values_t[:, sphere.rows(i)] = blocks[i][2].T
            grads_t[:, sphere.rows(i)] = blocks[i][3].T
    copy.wait()
    row, col, core = (lax.axis_index(a) for a in ("lat", "lon", "head"))
    limits = [
        counts[tuple(partner(row, col, core, n, lat, lon, True))] for n in range(tiles)
    ]
    sphere.mark(in_slots(limits))
    best, total = [None] * rounds, [None] * rounds

    def score(t, u):
        part = sphere.score(t, u)
        scores[t, sphere.lanes(u), :] = part
        best[t] = greater(best[t], sphere.folded(part, jnp.max))

    for u in range(rounds):
        score(0, u)
    for t in range(rounds):
        best[t] = jnp.max(best[t], axis=0, keepdims=True)
        for u in range(rounds):
            part = sphere.exponential(scores[t, sphere.lanes(u), :], best[t])
            scores[t, sphere.lanes(u), :] = part
            total[t] = sphere.added(total[t], t, u, part)
            if t + 1 < rounds:
                score(t + 1, u)
        stats[t, :8, :] = jnp.broadcast_to(best[t], (8, sphere.wide))
        stats[t, 8:, :] = total[t]


def finish_kernel(lat, lon, times, *refs):
    tiles = lat * lon
    blocks, refs = refs[:tiles], refs[tiles:]
    key_marks, query_marks, keys_t, values_t, grads_t, scores, grad_weights, stats = refs[:8]
    made, refs = refs[8 : 8 + tiles], refs[8 + tiles :]
    last_keys_t, last_values_t, last_grads_t, more_scores, weights_low, grads_low = refs
    sphere = Sphere(lat, lon, times, key_marks, query_marks)
    sphere.held[:] = blocks
    f32, low = jnp.float32, weights_low.dtype
    rounds, last = sphere.rounds, sphere.rounds - 1
    best, total, old, share, out_dot = ([None] * rounds for _ in range(5))
    early = slice(0, last * sphere.wide)
    late = sphere.lanes(last)

    def held_scores(t, j):
        if t < last and j // 2 < last:
            return scores.at[t, sphere.rows(j), :]
        if t < last:
            return more_scores.at[t, sphere.rows(j - 2 * last), :]
        return more_scores.at[last + j // 2, sphere.rows(j % 2), :]

    def score(t, u):
        part = sphere.score(t, u)
        for k in range(2):
            held_scores(t, 2 * u + k)[...] = part[sphere.rows(k), :]
        best[t] = greater(best[t], sphere.folded(part, jnp.max))

    def exponential(t, u):
        parts = []
        for j in (2 * u, 2 * u + 1):
            parts.append(sphere.exponential(held_scores(t, j)[...], best[t]))
            held_scores(t, j)[...] = parts[-1]
        total[t] = sphere.added(total[t], t, u, jnp.concatenate(parts, 0))

    def settle(t):
        before = stats[t, :1, :]
        best[t] = jnp.maximum(before, jnp.max(best[t], axis=0, keepdims=True))
        old[t] = sphere.exponential(before, best[t])
        total[t] = stats[t, 8:, :] * old[t]
        exponential(t, last)
        share[t] = 1.0 / jnp.sum(total[t], axis=0, keepdims=True)

    def factor(t, j):
        line = share[t] * sphere.named(t, j)
        return line * old[t] if t < last and j // 2 < last else line

    def weight(t, u):
        for j in (2 * u, 2 * u + 1):
            part = held_scores(t, j)[...] * factor(t, j)
            weights_low[sphere.rows(j), sphere.lanes(t)] = part.astype(low)

    def from_keys(first_t, last_t, low_scores, t):
        lanes = sphere.lanes(t)
        return jnp.dot(
            first_t[...], low_scores[early, lanes], preferred_element_type=f32
        ) + jnp.dot(last_t[...], low_scores[late, lanes], preferred_element_type=f32)

    def attend(t):
        out_t = from_keys(values_t, last_values_t, weights_low, t).astype(low)
        grad_t = grads_t[:, sphere.lanes(t)] if t < last else last_grads_t[...]
        out_dot[t] = jnp.sum(grad_t.astype(f32) * out_t.astype(f32), axis=0, keepdims=True)
        for k in range(2):
            made[2 * t + k][0] = out_t[:, sphere.rows(k)].T

    def grad_score(t, u):
        if t < last and u < last:
            part = grad_weights[t, sphere.lanes(u), :]
        else:
            part = sphere.grad_weight(t, u)
        for k in range(2):
            j = 2 * u + k
            weights = held_scores(t, j)[...] * factor(t, j)
            grad = weights * (part[sphere.rows(k), :] - out_dot[t])
            grads_low[sphere.rows(j), sphere.lanes(t)] = grad.astype(low)

    def query_grad(t):
        query_t = (from_keys(keys_t, last_keys_t, grads_low, t) * sphere.scale).astype(low)
        for k in range(2):
            made[2 * t + k][1] = query_t[:, sphere.rows(k)].T

    def key_side(n, low_scores, to, factor):
        part = jnp.dot(
            low_scores[...],
            jnp.concatenate([block[n] for block in blocks], 0),
            preferred_element_type=f32,
        )
        for j in range(tiles):
            made[j][to] = (part[sphere.rows(j), :] * factor).astype(low)

    for t in range(last):
        score(t, last)
    for k in range(2):
        block = blocks[2 * last + k]
        last_keys_t[:, sphere.rows(k)] = block[1].T
        last_values_t[:, sphere.rows(k)] = block[2].T
        last_grads_t[:, sphere.rows(k)] = block[3].T
    for t in range(last):
        settle(t)
        if t > 0:
            attend(t - 1)
        if t > 1:
            query_grad(t - 2)
        for u in range(rounds):
            weight(t, u)
            if t == 0:
                score(last, u)
            if t == 1 or last == 1:
                if u == 0:
                    best[last] = jnp.max(best[last], axis=0, keepdims=True)
                exponential(last, u)
            if t > 0:
                grad_score(t - 1, u)
    share[last] = 1.0 / jnp.sum(total[last], axis=0, keepdims=True)
    attend(last - 1)
    if last > 1:
        query_grad(last - 2)
    for u in range(rounds):
        weight(last, u)
        grad_score(last - 1, u)
    attend(last)
    key_side(3, weights_low, 3, 1.0)
    query_grad(last - 1)
    for u in range(rounds):
        grad_score(last, u)
    query_grad(last)
    key_side(0, grads_low, 2, sphere.scale)


def by_heads(queries, key_tokens, value_tokens, out_grad, counts):
    lat, lon, cores = (lax.axis_size(a) for a in ("lat", "lon", "head"))
    tiles = lat * lon
    tile_len, width = queries.shape[2], queries.shape[3]
    heads = width // HD
    low, f32 = queries.dtype, jnp.float32
    in_vmem = pl.BlockSpec(memory_space=pltpu.VMEM)
    in_hbm = pl.BlockSpec(memory_space=pltpu.HBM)
    whole = jax.ShapeDtypeStruct(queries.shape, low)
    block = pltpu.VMEM((4, tile_len, HD), low)
    small = pltpu.CompilerParams(vmem_limit_bytes=6 * 1024 * 1024)

    def sent(blocks, back):
        axes = ("lon", "lat", "head")
        moves = list(range(tiles - 1))
        if back:
            full, mixed, along = moves[:lat], moves[lat : 1 - lat], moves[1 - lat :]
            moves = full + along + mixed[::2] + mixed[1::2]
        found = list(blocks)
        for n in moves:
            found[n] = lax.ppermute(found[n], axes, routes(n, lat, lon, cores, heads, back))
        return found

    def from_hbm(*arrays):
        return [pltpu.with_memory_space_constraint(x, pltpu.HBM) for x in arrays]

    packed = pl.pallas_call(
        functools.partial(pack_kernel, lat, lon, heads),
        out_shape=[block] * tiles,
        in_specs=[in_hbm] * 4,
        out_specs=[in_vmem] * tiles,
        scratch_shapes=[
            pltpu.VMEM((4, tile_len, width), low),
            pltpu.SemaphoreType.DMA((4, 4)),
        ],
        compiler_params=small,
        name="pack",
    )(*from_hbm(queries, key_tokens, value_tokens, out_grad))
    there = in_slots(sent(packed, False))
    key_len, wide, begun = tiles * tile_len, 2 * tile_len, (tiles - 2) * tile_len
    times = relative_counts(lat, lon)
    large = pltpu.CompilerParams(vmem_limit_bytes=24 * 1024 * 1024)
    shared = [
        pltpu.VMEM((tiles, tile_len, HD), low),
        pltpu.VMEM((tiles, tile_len, HD), low),
        pltpu.VMEM((HD, begun), low),
        pltpu.VMEM((HD, begun), low),
        pltpu.VMEM((HD, begun), low),
        pltpu.VMEM((tiles // 2 - 1, begun, wide), f32),
        pltpu.VMEM((tiles // 2 - 1, begun, wide), f32),
        pltpu.VMEM((tiles // 2 - 1, 16, wide), f32),
    ]
    done = pl.pallas_call(
        functools.partial(begin_kernel, lat, lon, times),
        out_shape=shared,
        in_specs=[in_hbm] + [in_vmem] * (tiles - 2),
        out_specs=[in_vmem] * len(shared),
        scratch_shapes=[pltpu.SMEM(counts.shape, counts.dtype), pltpu.SemaphoreType.DMA],
        compiler_params=large,
        cost_estimate=pl.CostEstimate(
            flops=6 * begun * begun * HD,
            bytes_accessed=8 * begun * HD,
            transcendentals=begun * begun,
        ),
        name="begin",
    )(*from_hbm(counts), *there[: tiles - 2])
    made = pl.pallas_call(
        functools.partial(finish_kernel, lat, lon, times),
        out_shape=[block] * tiles,
        in_specs=[in_vmem] * (tiles + len(shared)),
        out_specs=[in_vmem] * tiles,
        scratch_shapes=[
            pltpu.VMEM((HD, wide), low),
            pltpu.VMEM((HD, wide), low),
            pltpu.VMEM((HD, wide), low),
            pltpu.VMEM((tiles - 1, wide, wide), f32),
            pltpu.VMEM((key_len, key_len), low),
            pltpu.VMEM((key_len, key_len), low),
        ],
        compiler_params=large,
        cost_estimate=pl.CostEstimate(
            flops=14 * key_len * key_len * HD - 6 * begun * begun * HD,
            bytes_accessed=16 * key_len * HD,
            transcendentals=key_len * key_len - begun * begun,
        ),
        name="finish",
    )(*there, *done)
    home = sent(in_steps(made), True)
    return tuple(
        pl.pallas_call(
            functools.partial(unpack_kernel, lat, lon, heads),
            out_shape=[whole] * 4,
            in_specs=[in_vmem] * tiles,
            out_specs=[in_hbm] * 4,
            scratch_shapes=[
                pltpu.VMEM((4, tile_len, width), low),
                pltpu.SemaphoreType.DMA((4, 4)),
            ],
            compiler_params=small,
            name="unpack",
        )(*home)
    )


def solution(mesh):
    tokens = P(("groups", "lat"), "lon", None, "head")

    def on_device(queries, *rest):
        lat, lon = mesh.shape["lat"], mesh.shape["lon"]
        one_tile = queries.shape[:2] == (1, 1)
        if one_tile and heads_fit(lat, lon, queries.shape[3] // HD):
            return by_heads(queries, *rest)
        return by_tiles(queries, *rest)

    return jax.shard_map(
        on_device,
        mesh=mesh,
        in_specs=(tokens,) * 4 + (P("groups", None),),
        out_specs=(tokens,) * 4,
        check_vma=False,
    )
```

```python
import functools
import math

import jax
import jax.numpy as jnp
from jax import lax
from jax.experimental import pallas as pl
from jax.experimental.pallas import tpu as pltpu
from jax.sharding import PartitionSpec as P

HD = 128


def with_halo(cells, sides, width, closed):
    for axis, dim in sides:
        count = lax.axis_size(axis)
        ends = count if closed else count - 1
        head = lax.slice_in_dim(cells, 0, width, axis=dim)
        tail = lax.slice_in_dim(cells, cells.shape[dim] - width, cells.shape[dim], axis=dim)
        cells = jnp.concatenate(
            [
                lax.ppermute(tail, axis, [(i, (i + 1) % count) for i in range(ends)]),
                cells,
                lax.ppermute(head, axis, [((i + 1) % count, i) for i in range(ends)]),
            ],
            axis=dim,
        )
    return cells


def passed_along(block, axis, distance):
    devices = range(lax.axis_size(axis))
    route = [((i - distance) % len(devices), i) for i in devices]
    return lax.ppermute(block, axis, route)


def neighbour_tiles(row_at, col_at, lat_tiles, lon_tiles):
    row_step = jnp.array([-1, -1, -1, 0, 0, 0, 1, 1, 1], dtype=jnp.int32)
    col_step = jnp.array([-1, 0, 1, -1, 0, 1, -1, 0, 1], dtype=jnp.int32)
    row_next = row_at + row_step
    across = (row_next < 0) | (row_next > lat_tiles - 1)
    col_next = (col_at + col_step + jnp.where(across, lon_tiles // 2, 0)) % lon_tiles
    row_next = jnp.clip(row_next, 0, lat_tiles - 1)
    return row_next * lon_tiles + col_next


def close_poles(rim_block, mirror):
    lat_index = lax.axis_index("lat")
    last_index = lax.axis_size("lat") - 1
    north_rim = jnp.where(lat_index == 0, mirror, rim_block[:1])
    south_rim = jnp.where(lat_index == last_index, mirror, rim_block[-1:])
    return jnp.concatenate([north_rim, rim_block[1:-1], south_rim], 0)


def around_pair(first_block, second_block):
    row_faces = (
        with_halo(first_block, (("lat", 0),), 1, False),
        with_halo(second_block, (("lat", 0),), 1, False),
    )
    mirror = passed_along((first_block, second_block), "lon", lax.axis_size("lon") // 2)
    column_a = close_poles(row_faces[0], mirror[0])
    column_b = close_poles(row_faces[1], mirror[1])
    return (
        with_halo(column_a, (("lon", 1),), 1, True),
        with_halo(column_b, (("lon", 1),), 1, True),
    )


def around_stats(log_total, out_dot):
    near_stats = (
        with_halo(log_total, (("lon", 1), ("lat", 0)), 1, True),
        with_halo(out_dot, (("lon", 1), ("lat", 0)), 1, True),
    )
    own_rows = log_total.shape[0]
    own_total = near_stats[0][1 : own_rows + 1]
    own_dot = near_stats[1][1 : own_rows + 1]
    mirror = passed_along((own_total, own_dot), "lon", lax.axis_size("lon") // 2)
    return (close_poles(near_stats[0], mirror[0]), close_poles(near_stats[1], mirror[1]))


def by_tiles(queries, key_tokens, value_tokens, out_grad, counts):
    own_rows = queries.shape[0]
    tile_len = queries.shape[2]
    feat_width = queries.shape[3]
    head_count = feat_width // HD
    lat_tiles = counts.shape[0]
    lon_tiles = counts.shape[1]
    row_base = lax.axis_index("lat") * own_rows
    col_at = lax.axis_index("lon")
    score_scale = 1.0 / math.sqrt(HD)
    positions = jnp.arange(tile_len, dtype=jnp.int32)
    flat_counts = counts.reshape(-1)
    near_k, near_v = around_pair(key_tokens, value_tokens)
    slot_ids = neighbour_tiles(row_base, col_at, lat_tiles, lon_tiles)
    key_valid = (positions[None, :] < flat_counts[slot_ids][:, None]).reshape(-1)
    near_keys = near_k.reshape(9 * tile_len, feat_width)
    near_values = near_v.reshape(9 * tile_len, feat_width)
    head_outs = []
    query_parts = []
    head_totals = []
    head_dots = []
    for head_index in range(head_count):
        columns = slice(head_index * HD, (head_index + 1) * HD)
        query_here = queries[0, 0, :, columns]
        grad_here = out_grad[0, 0, :, columns]
        keys_head = near_keys[:, columns]
        values_head = near_values[:, columns]
        scores = (
            jnp.einsum("qd,kd->qk", query_here, keys_head, preferred_element_type=jnp.float32)
            * score_scale
        )
        row_max = jnp.max(jnp.where(key_valid[None, :], scores, -1e30), axis=-1, keepdims=True)
        row_total = jnp.sum(
            jnp.where(key_valid[None, :], jnp.exp(scores - row_max), 0.0), axis=-1, keepdims=True
        )
        log_total = row_max + jnp.log(row_total)
        weights = jnp.where(key_valid[None, :], jnp.exp(scores - log_total), 0.0)
        weights_low = weights.astype(jnp.bfloat16)
        head_out = jnp.dot(weights_low, values_head, preferred_element_type=jnp.float32).astype(
            jnp.bfloat16
        )
        out_dot = jnp.sum(grad_here.astype(jnp.float32) * head_out.astype(jnp.float32), axis=-1)
        grad_weights = jnp.einsum(
            "qd,kd->qk", grad_here, values_head, preferred_element_type=jnp.float32
        )
        grad_scores = (weights * (grad_weights - out_dot[:, None])).astype(jnp.bfloat16)
        query_part = (
            jnp.dot(grad_scores, keys_head, preferred_element_type=jnp.float32) * score_scale
        )
        head_outs.append(head_out)
        query_parts.append(query_part.astype(jnp.bfloat16))
        head_totals.append(log_total[:, 0])
        head_dots.append(out_dot)
    attended = jnp.concatenate(head_outs, -1)[None, None]
    query_grad = jnp.concatenate(query_parts, -1)[None, None]
    own_totals = jnp.stack(head_totals)[None, None]
    own_dots = jnp.stack(head_dots)[None, None]
    near_q, near_g = around_pair(queries, out_grad)
    near_total, near_dot = around_stats(own_totals, own_dots)
    own_valid = positions < counts[row_base, col_at]
    near_queries = near_q.reshape(9 * tile_len, feat_width)
    near_grads = near_g.reshape(9 * tile_len, feat_width)
    key_parts = []
    value_parts = []
    for head_index in range(head_count):
        columns = slice(head_index * HD, (head_index + 1) * HD)
        queries_head = near_queries[:, columns]
        grads_head = near_grads[:, columns]
        keys_here = key_tokens[0, 0, :, columns]
        values_here = value_tokens[0, 0, :, columns]
        totals_head = near_total[:, :, head_index, :].reshape(9 * tile_len)
        dots_head = near_dot[:, :, head_index, :].reshape(9 * tile_len)
        scores = (
            jnp.einsum("qd,kd->qk", queries_head, keys_here, preferred_element_type=jnp.float32)
            * score_scale
        )
        weights = jnp.where(own_valid[None, :], jnp.exp(scores - totals_head[:, None]), 0.0)
        weights_low = weights.astype(jnp.bfloat16)
        value_part = jnp.einsum(
            "qk,qd->kd", weights_low, grads_head, preferred_element_type=jnp.float32
        )
        grad_weights = jnp.einsum(
            "qd,kd->qk", grads_head, values_here, preferred_element_type=jnp.float32
        )
        grad_scores = (weights * (grad_weights - dots_head[:, None])).astype(jnp.bfloat16)
        key_part = (
            jnp.einsum("qk,qd->kd", grad_scores, queries_head, preferred_element_type=jnp.float32)
            * score_scale
        )
        key_parts.append(key_part.astype(jnp.bfloat16))
        value_parts.append(value_part.astype(jnp.bfloat16))
    key_grad = jnp.concatenate(key_parts, -1)[None, None]
    value_grad = jnp.concatenate(value_parts, -1)[None, None]
    return (attended, query_grad, key_grad, value_grad)


def heads_fit(lat, lon, heads):
    fits = (
        heads % lat == 0
        and heads // lat <= lon <= 2 * (heads // lat)
        and lon % 2 == 0
        and 4 <= lat * lon <= 16
    )
    if not fits:
        return False
    first = relative_counts(lat, lon)
    return all(
        relative_counts(lat, lon, row, col, core) == first
        for row in range(lat)
        for col in range(lon)
        for core in range(2)
    )


def relative_counts(lat, lon, row=0, col=0, core=0):
    times = slot_counts(lat, lon)
    tile = []
    for step in steps_of(lat, lon, core):
        from_col = [c for c in range(lon) if column_after(c, step, lon) == col][0]
        tile.append((row - step[1]) % lat * lon + from_col)
    tile = in_slots(tile)
    return [[times[i][j] for j in tile] for i in tile]


def in_slots(found):
    return [*found[:-3], found[-1], *found[-3:-1]]


def in_steps(found):
    return [*found[:-3], *found[-2:], found[-3]]


def head_of(row, col, core, lat, lon, heads):
    per_row = heads // lat
    place = col - (1 - core % 2) * (lon - per_row)
    return row * per_row + place, (place >= 0) & (place < per_row)


def steps_of(lat, lon, core):
    half = lon // 2
    found = [(True, row_step, 0) for row_step in range(lat - 1, -1, -1)]
    for row_step in range(lat - 1, -1, -1):
        for col_step in range(1, half):
            turns = (True, row_step, col_step), (False, row_step, col_step)
            found.extend(turns[::-1] if core % 2 else turns)
    found.extend((False, row_step, 0) for row_step in range(1, lat))
    return found + [(False, 0, 0)]


def column_after(col, step, lon):
    half = lon // 2
    other = col // half ^ int(step[0])
    return other * half + (col + step[2]) % half


def partner(row, col, core, n, lat, lon, back=False):
    places = []
    for which in (0, 1):
        step = steps_of(lat, lon, which)[n]
        to_row = lax.rem(row + (lat - step[1] if back else step[1]), lat)
        to_col = jnp.int32(0)
        for here in range(lon):
            there = column_after(here, step, lon)
            if back:
                to_col = jnp.where(col == there, here, to_col)
            else:
                to_col = jnp.where(col == here, there, to_col)
        places.append((to_row, to_col))
    return [jnp.where(core % 2 == 0, a, b) for a, b in zip(*places)]


def routes(n, lat, lon, cores, heads, back):
    pairs = []
    for row in range(lat):
        for col in range(lon):
            for core in range(cores):
                step = steps_of(lat, lon, core)[n]
                to_row, to_col = (row + step[1]) % lat, column_after(col, step, lon)
                if head_of(to_row, to_col, core, lat, lon, heads)[1]:
                    here = (col * lat + row) * cores + core
                    there = (to_col * lat + to_row) * cores + core
                    pairs.append((there, here) if back else (here, there))
    return pairs


def slot_counts(lat, lon):
    times = [[0] * (lat * lon) for _ in range(lat * lon)]
    for row in range(lat):
        for col in range(lon):
            for a in (-1, 0, 1):
                for b in (-1, 0, 1):
                    near_row, near_col = row + a, col + b
                    if near_row < 0 or near_row > lat - 1:
                        near_col += lon // 2
                        near_row = min(max(near_row, 0), lat - 1)
                    times[row * lon + col][near_row * lon + near_col % lon] += 1
    return times


def pack_kernel(lat, lon, heads, *refs):
    tensors, blocks, whole, sems = refs[:4], refs[4:-2], refs[-2], refs[-1]
    row, col, core = (lax.axis_index(a) for a in ("lat", "lon", "head"))
    parts = sems.shape[1]
    size = whole.shape[1] // parts
    copies = []
    for n in range(parts):
        rows = pl.ds(n * size, size)
        for t, tensor in enumerate(tensors):
            copies.append(
                pltpu.make_async_copy(
                    tensor.at[0, 0, rows, :], whole.at[t, rows, :], sems.at[t, n]
                )
            )
    for copy in copies:
        copy.start()
    for n in range(parts):
        rows = slice(n * size, (n + 1) * size)
        for copy in copies[4 * n : 4 * n + 4]:
            copy.wait()
        for m, block in enumerate(blocks):
            head, used = head_of(*partner(row, col, core, m, lat, lon), core, lat, lon, heads)

            @pl.when(used)
            def _():
                features = pl.ds(pl.multiple_of(head * HD, HD), HD)
                for t in range(4):
                    block[t, rows, :] = whole[t, rows, features]


def unpack_kernel(lat, lon, heads, *refs):
    blocks, tensors, whole, sems = refs[:-6], refs[-6:-2], refs[-2], refs[-1]
    row, col, core = (lax.axis_index(a) for a in ("lat", "lon", "head"))
    copies = []
    for t, tensor in enumerate(tensors):
        for m, block in enumerate(blocks):
            head, used = head_of(*partner(row, col, core, m, lat, lon), core, lat, lon, heads)

            @pl.when(used)
            def _():
                features = pl.ds(pl.multiple_of(head * HD, HD), HD)
                whole[t, :, features] = block[t]

        copies.append(pltpu.make_async_copy(whole.at[t], tensor.at[0, 0], sems.at[t]))
        copies[-1].start()
    for copy in copies:
        copy.wait()


class Sphere:
    def __init__(self, lat, lon, times, key_marks, query_marks):
        self.tiles = lat * lon
        self.times = times
        self.key_marks, self.query_marks = key_marks, query_marks
        self.size = key_marks.shape[1]
        self.wide = 2 * self.size
        self.rounds = self.tiles // 2
        self.scale = 1.0 / math.sqrt(HD)
        self.of_tile = lax.broadcasted_iota(jnp.int32, (1, self.wide), 1) // self.size
        self.held = [None] * self.tiles

    def mark(self, limits):
        shape = (self.size, HD)
        key_row = lax.broadcasted_iota(jnp.int32, shape, 0)
        lane = lax.broadcasted_iota(jnp.int32, shape, 1)
        for j in range(self.tiles):
            unseen = (lane == 0) & (key_row >= limits[j])
            key_mark = jnp.where(unseen, -1e30, jnp.where(lane == j + 1, 1.0, 0.0))
            self.key_marks[j] = key_mark.astype(self.key_marks.dtype)
            apart = jnp.zeros(shape, jnp.bool_)
            for k in range(self.tiles):
                if self.times[j][k] == 0:
                    apart = apart | (lane == k + 1)
            query_mark = jnp.where(apart, -1e30, jnp.where(lane == 0, 1.0, 0.0))
            self.query_marks[j] = query_mark.astype(self.query_marks.dtype)

    def rows(self, j):
        return slice(j * self.size, (j + 1) * self.size)

    def lanes(self, t):
        return slice(t * self.wide, (t + 1) * self.wide)

    def stacked(self, t, n):
        return jnp.concatenate([self.held[2 * t + k][n] for k in range(2)], 0)

    def marked(self, t, n, marks):
        parts = [(self.held[i][n], marks[i]) for i in (2 * t, 2 * t + 1)]
        return jnp.concatenate([jnp.concatenate(part, 1) for part in parts], 0)

    def score(self, t, u):
        return contract_last(
            self.marked(u, 1, self.key_marks), self.marked(t, 0, self.query_marks)
        )

    def grad_weight(self, t, u):
        return contract_last(self.stacked(u, 2), self.stacked(t, 3))

    def exponential(self, scores, top):
        return jnp.exp2((scores - top) * (self.scale * math.log2(math.e)))

    def named(self, t, j):
        line = jnp.ones((1, self.wide), jnp.float32)
        for k in range(2):
            if self.times[2 * t + k][j] > 1:
                line = jnp.where(self.of_tile == k, float(self.times[2 * t + k][j]), line)
        return line

    def folded(self, part, op):
        return op(part.reshape(part.shape[0] // 8, 8, self.wide), axis=0)

    def added(self, total, t, u, parts):
        for k in range(2):
            part = self.folded(parts[self.rows(k), :], jnp.sum) * self.named(t, 2 * u + k)
            total = part if total is None else total + part
        return total


def contract_last(a, b):
    return lax.dot_general(a, b, (((1,), (1,)), ((), ())), preferred_element_type=jnp.float32)


def greater(a, b):
    return b if a is None else jnp.maximum(a, b)


def begin_kernel(lat, lon, times, *refs):
    tiles = lat * lon
    all_counts, blocks, outs = refs[0], refs[1 : tiles - 1], refs[tiles - 1 :]
    key_marks, query_marks, keys_t, values_t, grads_t, scores, grad_weights, stats = outs[:8]
    counts, sem = outs[8:]
    sphere = Sphere(lat, lon, times, key_marks, query_marks)
    sphere.held[: tiles - 2] = blocks
    rounds = sphere.rounds - 1
    copy = pltpu.make_async_copy(all_counts, counts, sem)
    copy.start()
    for t in range(rounds):
        for u in range(rounds):
            grad_weights[t, sphere.lanes(u), :] = sphere.grad_weight(t, u)
        for i in (2 * t, 2 * t + 1):
            keys_t[:, sphere.rows(i)] = blocks[i][1].T
            values_t[:, sphere.rows(i)] = blocks[i][2].T
            grads_t[:, sphere.rows(i)] = blocks[i][3].T
    copy.wait()
    row, col, core = (lax.axis_index(a) for a in ("lat", "lon", "head"))
    limits = [
        counts[tuple(partner(row, col, core, n, lat, lon, True))] for n in range(tiles)
    ]
    sphere.mark(in_slots(limits))
    best, total = [None] * rounds, [None] * rounds

    def score(t, u):
        part = sphere.score(t, u)
        scores[t, sphere.lanes(u), :] = part
        best[t] = greater(best[t], sphere.folded(part, jnp.max))

    for u in range(rounds):
        score(0, u)
    for t in range(rounds):
        best[t] = jnp.max(best[t], axis=0, keepdims=True)
        for u in range(rounds):
            part = sphere.exponential(scores[t, sphere.lanes(u), :], best[t])
            scores[t, sphere.lanes(u), :] = part
            total[t] = sphere.added(total[t], t, u, part)
            if t + 1 < rounds:
                score(t + 1, u)
        stats[t, :8, :] = jnp.broadcast_to(best[t], (8, sphere.wide))
        stats[t, 8:, :] = total[t]


def finish_kernel(lat, lon, times, *refs):
    tiles = lat * lon
    blocks, refs = refs[:tiles], refs[tiles:]
    key_marks, query_marks, keys_t, values_t, grads_t, scores, grad_weights, stats = refs[:8]
    made, refs = refs[8 : 8 + tiles], refs[8 + tiles :]
    last_keys_t, last_values_t, last_grads_t, more_scores, weights_low, grads_low = refs
    sphere = Sphere(lat, lon, times, key_marks, query_marks)
    sphere.held[:] = blocks
    f32, low = jnp.float32, weights_low.dtype
    rounds, last = sphere.rounds, sphere.rounds - 1
    best, total, old, share, out_dot = ([None] * rounds for _ in range(5))
    early = slice(0, last * sphere.wide)
    late = sphere.lanes(last)

    def held_scores(t, j):
        if t < last and j // 2 < last:
            return scores.at[t, sphere.rows(j), :]
        if t < last:
            return more_scores.at[t, sphere.rows(j - 2 * last), :]
        return more_scores.at[last + j // 2, sphere.rows(j % 2), :]

    def score(t, u):
        part = sphere.score(t, u)
        for k in range(2):
            held_scores(t, 2 * u + k)[...] = part[sphere.rows(k), :]
        best[t] = greater(best[t], sphere.folded(part, jnp.max))

    def exponential(t, u):
        parts = []
        for j in (2 * u, 2 * u + 1):
            parts.append(sphere.exponential(held_scores(t, j)[...], best[t]))
            held_scores(t, j)[...] = parts[-1]
        total[t] = sphere.added(total[t], t, u, jnp.concatenate(parts, 0))

    def settle(t):
        before = stats[t, :1, :]
        best[t] = jnp.maximum(before, jnp.max(best[t], axis=0, keepdims=True))
        old[t] = sphere.exponential(before, best[t])
        total[t] = stats[t, 8:, :] * old[t]
        exponential(t, last)
        share[t] = 1.0 / jnp.sum(total[t], axis=0, keepdims=True)

    def factor(t, j):
        line = share[t] * sphere.named(t, j)
        return line * old[t] if t < last and j // 2 < last else line

    def weight(t, u):
        for j in (2 * u, 2 * u + 1):
            part = held_scores(t, j)[...] * factor(t, j)
            weights_low[sphere.rows(j), sphere.lanes(t)] = part.astype(low)

    def from_keys(first_t, last_t, low_scores, t):
        lanes = sphere.lanes(t)
        return jnp.dot(
            first_t[...], low_scores[early, lanes], preferred_element_type=f32
        ) + jnp.dot(last_t[...], low_scores[late, lanes], preferred_element_type=f32)

    def attend(t):
        out_t = from_keys(values_t, last_values_t, weights_low, t).astype(low)
        grad_t = grads_t[:, sphere.lanes(t)] if t < last else last_grads_t[...]
        out_dot[t] = jnp.sum(grad_t.astype(f32) * out_t.astype(f32), axis=0, keepdims=True)
        for k in range(2):
            made[2 * t + k][0] = out_t[:, sphere.rows(k)].T

    def grad_score(t, u):
        if t < last and u < last:
            part = grad_weights[t, sphere.lanes(u), :]
        else:
            part = sphere.grad_weight(t, u)
        for k in range(2):
            j = 2 * u + k
            weights = held_scores(t, j)[...] * factor(t, j)
            grad = weights * (part[sphere.rows(k), :] - out_dot[t])
            grads_low[sphere.rows(j), sphere.lanes(t)] = grad.astype(low)

    def query_grad(t):
        query_t = (from_keys(keys_t, last_keys_t, grads_low, t) * sphere.scale).astype(low)
        for k in range(2):
            made[2 * t + k][1] = query_t[:, sphere.rows(k)].T

    def key_side(n, low_scores, to, factor):
        part = jnp.dot(
            low_scores[...],
            jnp.concatenate([block[n] for block in blocks], 0),
            preferred_element_type=f32,
        )
        for j in range(tiles):
            made[j][to] = (part[sphere.rows(j), :] * factor).astype(low)

    for t in range(last):
        score(t, last)
    for k in range(2):
        block = blocks[2 * last + k]
        last_keys_t[:, sphere.rows(k)] = block[1].T
        last_values_t[:, sphere.rows(k)] = block[2].T
        last_grads_t[:, sphere.rows(k)] = block[3].T
    for t in range(last):
        settle(t)
        if t > 0:
            attend(t - 1)
        if t > 1:
            query_grad(t - 2)
        for u in range(rounds):
            weight(t, u)
            if t == 0:
                score(last, u)
            if t == 1 or last == 1:
                if u == 0:
                    best[last] = jnp.max(best[last], axis=0, keepdims=True)
                exponential(last, u)
            if t > 0:
                grad_score(t - 1, u)
    share[last] = 1.0 / jnp.sum(total[last], axis=0, keepdims=True)
    attend(last - 1)
    if last > 1:
        query_grad(last - 2)
    for u in range(rounds):
        weight(last, u)
        grad_score(last - 1, u)
    attend(last)
    key_side(3, weights_low, 3, 1.0)
    query_grad(last - 1)
    for u in range(rounds):
        grad_score(last, u)
    query_grad(last)
    key_side(0, grads_low, 2, sphere.scale)


def by_heads(queries, key_tokens, value_tokens, out_grad, counts):
    lat, lon, cores = (lax.axis_size(a) for a in ("lat", "lon", "head"))
    tiles = lat * lon
    tile_len, width = queries.shape[2], queries.shape[3]
    heads = width // HD
    low, f32 = queries.dtype, jnp.float32
    in_vmem = pl.BlockSpec(memory_space=pltpu.VMEM)
    in_hbm = pl.BlockSpec(memory_space=pltpu.HBM)
    whole = jax.ShapeDtypeStruct(queries.shape, low)
    block = pltpu.VMEM((4, tile_len, HD), low)
    small = pltpu.CompilerParams(vmem_limit_bytes=6 * 1024 * 1024)

    def sent(blocks, back):
        axes = ("lon", "lat", "head")
        moves = list(range(tiles - 1))
        if back:
            full, mixed, along = moves[:lat], moves[lat : 1 - lat], moves[1 - lat :]
            moves = full + mixed[::2] + mixed[1::2] + along
        found = list(blocks)
        for n in moves:
            found[n] = lax.ppermute(found[n], axes, routes(n, lat, lon, cores, heads, back))
        return found

    def from_hbm(*arrays):
        return [pltpu.with_memory_space_constraint(x, pltpu.HBM) for x in arrays]

    packed = pl.pallas_call(
        functools.partial(pack_kernel, lat, lon, heads),
        out_shape=[block] * tiles,
        in_specs=[in_hbm] * 4,
        out_specs=[in_vmem] * tiles,
        scratch_shapes=[
            pltpu.VMEM((4, tile_len, width), low),
            pltpu.SemaphoreType.DMA((4, 4)),
        ],
        compiler_params=small,
        name="pack",
    )(*from_hbm(queries, key_tokens, value_tokens, out_grad))
    there = in_slots(sent(packed, False))
    key_len, wide, begun = tiles * tile_len, 2 * tile_len, (tiles - 2) * tile_len
    times = relative_counts(lat, lon)
    large = pltpu.CompilerParams(vmem_limit_bytes=24 * 1024 * 1024)
    shared = [
        pltpu.VMEM((tiles, tile_len, HD), low),
        pltpu.VMEM((tiles, tile_len, HD), low),
        pltpu.VMEM((HD, begun), low),
        pltpu.VMEM((HD, begun), low),
        pltpu.VMEM((HD, begun), low),
        pltpu.VMEM((tiles // 2 - 1, begun, wide), f32),
        pltpu.VMEM((tiles // 2 - 1, begun, wide), f32),
        pltpu.VMEM((tiles // 2 - 1, 16, wide), f32),
    ]
    done = pl.pallas_call(
        functools.partial(begin_kernel, lat, lon, times),
        out_shape=shared,
        in_specs=[in_hbm] + [in_vmem] * (tiles - 2),
        out_specs=[in_vmem] * len(shared),
        scratch_shapes=[pltpu.SMEM(counts.shape, counts.dtype), pltpu.SemaphoreType.DMA],
        compiler_params=large,
        cost_estimate=pl.CostEstimate(
            flops=6 * begun * begun * HD,
            bytes_accessed=8 * begun * HD,
            transcendentals=begun * begun,
        ),
        name="begin",
    )(*from_hbm(counts), *there[: tiles - 2])
    made = pl.pallas_call(
        functools.partial(finish_kernel, lat, lon, times),
        out_shape=[block] * tiles,
        in_specs=[in_vmem] * (tiles + len(shared)),
        out_specs=[in_vmem] * tiles,
        scratch_shapes=[
            pltpu.VMEM((HD, wide), low),
            pltpu.VMEM((HD, wide), low),
            pltpu.VMEM((HD, wide), low),
            pltpu.VMEM((tiles - 1, wide, wide), f32),
            pltpu.VMEM((key_len, key_len), low),
            pltpu.VMEM((key_len, key_len), low),
        ],
        compiler_params=large,
        cost_estimate=pl.CostEstimate(
            flops=14 * key_len * key_len * HD - 6 * begun * begun * HD,
            bytes_accessed=16 * key_len * HD,
            transcendentals=key_len * key_len - begun * begun,
        ),
        name="finish",
    )(*there, *done)
    home = sent(in_steps(made), True)
    return tuple(
        pl.pallas_call(
            functools.partial(unpack_kernel, lat, lon, heads),
            out_shape=[whole] * 4,
            in_specs=[in_vmem] * tiles,
            out_specs=[in_hbm] * 4,
            scratch_shapes=[
                pltpu.VMEM((4, tile_len, width), low),
                pltpu.SemaphoreType.DMA((4,)),
            ],
            compiler_params=small,
            name="unpack",
        )(*home)
    )


def solution(mesh):
    tokens = P(("groups", "lat"), "lon", None, "head")

    def on_device(queries, *rest):
        lat, lon = mesh.shape["lat"], mesh.shape["lon"]
        one_tile = queries.shape[:2] == (1, 1)
        if one_tile and heads_fit(lat, lon, queries.shape[3] // HD):
            return by_heads(queries, *rest)
        return by_tiles(queries, *rest)

    return jax.shard_map(
        on_device,
        mesh=mesh,
        in_specs=(tokens,) * 4 + (P("groups", None),),
        out_specs=(tokens,) * 4,
        check_vma=False,
    )
```

```python
import functools
import math

import jax
import jax.numpy as jnp
from jax import lax
from jax.experimental import pallas as pl
from jax.experimental.pallas import tpu as pltpu
from jax.sharding import PartitionSpec as P

HD = 128


def with_halo(cells, sides, width, closed):
    for axis, dim in sides:
        count = lax.axis_size(axis)
        ends = count if closed else count - 1
        head = lax.slice_in_dim(cells, 0, width, axis=dim)
        tail = lax.slice_in_dim(cells, cells.shape[dim] - width, cells.shape[dim], axis=dim)
        cells = jnp.concatenate(
            [
                lax.ppermute(tail, axis, [(i, (i + 1) % count) for i in range(ends)]),
                cells,
                lax.ppermute(head, axis, [((i + 1) % count, i) for i in range(ends)]),
            ],
            axis=dim,
        )
    return cells


def passed_along(block, axis, distance):
    devices = range(lax.axis_size(axis))
    route = [((i - distance) % len(devices), i) for i in devices]
    return lax.ppermute(block, axis, route)


def neighbour_tiles(row_at, col_at, lat_tiles, lon_tiles):
    row_step = jnp.array([-1, -1, -1, 0, 0, 0, 1, 1, 1], dtype=jnp.int32)
    col_step = jnp.array([-1, 0, 1, -1, 0, 1, -1, 0, 1], dtype=jnp.int32)
    row_next = row_at + row_step
    across = (row_next < 0) | (row_next > lat_tiles - 1)
    col_next = (col_at + col_step + jnp.where(across, lon_tiles // 2, 0)) % lon_tiles
    row_next = jnp.clip(row_next, 0, lat_tiles - 1)
    return row_next * lon_tiles + col_next


def close_poles(rim_block, mirror):
    lat_index = lax.axis_index("lat")
    last_index = lax.axis_size("lat") - 1
    north_rim = jnp.where(lat_index == 0, mirror, rim_block[:1])
    south_rim = jnp.where(lat_index == last_index, mirror, rim_block[-1:])
    return jnp.concatenate([north_rim, rim_block[1:-1], south_rim], 0)


def around_pair(first_block, second_block):
    row_faces = (
        with_halo(first_block, (("lat", 0),), 1, False),
        with_halo(second_block, (("lat", 0),), 1, False),
    )
    mirror = passed_along((first_block, second_block), "lon", lax.axis_size("lon") // 2)
    column_a = close_poles(row_faces[0], mirror[0])
    column_b = close_poles(row_faces[1], mirror[1])
    return (
        with_halo(column_a, (("lon", 1),), 1, True),
        with_halo(column_b, (("lon", 1),), 1, True),
    )


def around_stats(log_total, out_dot):
    near_stats = (
        with_halo(log_total, (("lon", 1), ("lat", 0)), 1, True),
        with_halo(out_dot, (("lon", 1), ("lat", 0)), 1, True),
    )
    own_rows = log_total.shape[0]
    own_total = near_stats[0][1 : own_rows + 1]
    own_dot = near_stats[1][1 : own_rows + 1]
    mirror = passed_along((own_total, own_dot), "lon", lax.axis_size("lon") // 2)
    return (close_poles(near_stats[0], mirror[0]), close_poles(near_stats[1], mirror[1]))


def by_tiles(queries, key_tokens, value_tokens, out_grad, counts):
    own_rows = queries.shape[0]
    tile_len = queries.shape[2]
    feat_width = queries.shape[3]
    head_count = feat_width // HD
    lat_tiles = counts.shape[0]
    lon_tiles = counts.shape[1]
    row_base = lax.axis_index("lat") * own_rows
    col_at = lax.axis_index("lon")
    score_scale = 1.0 / math.sqrt(HD)
    positions = jnp.arange(tile_len, dtype=jnp.int32)
    flat_counts = counts.reshape(-1)
    near_k, near_v = around_pair(key_tokens, value_tokens)
    slot_ids = neighbour_tiles(row_base, col_at, lat_tiles, lon_tiles)
    key_valid = (positions[None, :] < flat_counts[slot_ids][:, None]).reshape(-1)
    near_keys = near_k.reshape(9 * tile_len, feat_width)
    near_values = near_v.reshape(9 * tile_len, feat_width)
    head_outs = []
    query_parts = []
    head_totals = []
    head_dots = []
    for head_index in range(head_count):
        columns = slice(head_index * HD, (head_index + 1) * HD)
        query_here = queries[0, 0, :, columns]
        grad_here = out_grad[0, 0, :, columns]
        keys_head = near_keys[:, columns]
        values_head = near_values[:, columns]
        scores = (
            jnp.einsum("qd,kd->qk", query_here, keys_head, preferred_element_type=jnp.float32)
            * score_scale
        )
        row_max = jnp.max(jnp.where(key_valid[None, :], scores, -1e30), axis=-1, keepdims=True)
        row_total = jnp.sum(
            jnp.where(key_valid[None, :], jnp.exp(scores - row_max), 0.0), axis=-1, keepdims=True
        )
        log_total = row_max + jnp.log(row_total)
        weights = jnp.where(key_valid[None, :], jnp.exp(scores - log_total), 0.0)
        weights_low = weights.astype(jnp.bfloat16)
        head_out = jnp.dot(weights_low, values_head, preferred_element_type=jnp.float32).astype(
            jnp.bfloat16
        )
        out_dot = jnp.sum(grad_here.astype(jnp.float32) * head_out.astype(jnp.float32), axis=-1)
        grad_weights = jnp.einsum(
            "qd,kd->qk", grad_here, values_head, preferred_element_type=jnp.float32
        )
        grad_scores = (weights * (grad_weights - out_dot[:, None])).astype(jnp.bfloat16)
        query_part = (
            jnp.dot(grad_scores, keys_head, preferred_element_type=jnp.float32) * score_scale
        )
        head_outs.append(head_out)
        query_parts.append(query_part.astype(jnp.bfloat16))
        head_totals.append(log_total[:, 0])
        head_dots.append(out_dot)
    attended = jnp.concatenate(head_outs, -1)[None, None]
    query_grad = jnp.concatenate(query_parts, -1)[None, None]
    own_totals = jnp.stack(head_totals)[None, None]
    own_dots = jnp.stack(head_dots)[None, None]
    near_q, near_g = around_pair(queries, out_grad)
    near_total, near_dot = around_stats(own_totals, own_dots)
    own_valid = positions < counts[row_base, col_at]
    near_queries = near_q.reshape(9 * tile_len, feat_width)
    near_grads = near_g.reshape(9 * tile_len, feat_width)
    key_parts = []
    value_parts = []
    for head_index in range(head_count):
        columns = slice(head_index * HD, (head_index + 1) * HD)
        queries_head = near_queries[:, columns]
        grads_head = near_grads[:, columns]
        keys_here = key_tokens[0, 0, :, columns]
        values_here = value_tokens[0, 0, :, columns]
        totals_head = near_total[:, :, head_index, :].reshape(9 * tile_len)
        dots_head = near_dot[:, :, head_index, :].reshape(9 * tile_len)
        scores = (
            jnp.einsum("qd,kd->qk", queries_head, keys_here, preferred_element_type=jnp.float32)
            * score_scale
        )
        weights = jnp.where(own_valid[None, :], jnp.exp(scores - totals_head[:, None]), 0.0)
        weights_low = weights.astype(jnp.bfloat16)
        value_part = jnp.einsum(
            "qk,qd->kd", weights_low, grads_head, preferred_element_type=jnp.float32
        )
        grad_weights = jnp.einsum(
            "qd,kd->qk", grads_head, values_here, preferred_element_type=jnp.float32
        )
        grad_scores = (weights * (grad_weights - dots_head[:, None])).astype(jnp.bfloat16)
        key_part = (
            jnp.einsum("qk,qd->kd", grad_scores, queries_head, preferred_element_type=jnp.float32)
            * score_scale
        )
        key_parts.append(key_part.astype(jnp.bfloat16))
        value_parts.append(value_part.astype(jnp.bfloat16))
    key_grad = jnp.concatenate(key_parts, -1)[None, None]
    value_grad = jnp.concatenate(value_parts, -1)[None, None]
    return (attended, query_grad, key_grad, value_grad)


def heads_fit(lat, lon, heads):
    fits = (
        heads % lat == 0
        and heads // lat <= lon <= 2 * (heads // lat)
        and lon % 2 == 0
        and 4 <= lat * lon <= 16
    )
    if not fits:
        return False
    first = relative_counts(lat, lon)
    return all(
        relative_counts(lat, lon, row, col, core) == first
        for row in range(lat)
        for col in range(lon)
        for core in range(2)
    )


def relative_counts(lat, lon, row=0, col=0, core=0):
    times = slot_counts(lat, lon)
    tile = []
    for step in steps_of(lat, lon, core):
        from_col = [c for c in range(lon) if column_after(c, step, lon) == col][0]
        tile.append((row - step[1]) % lat * lon + from_col)
    tile = in_slots(tile)
    return [[times[i][j] for j in tile] for i in tile]


def in_slots(found):
    return [*found[:-3], found[-1], *found[-3:-1]]


def in_steps(found):
    return [*found[:-3], *found[-2:], found[-3]]


def head_of(row, col, core, lat, lon, heads):
    per_row = heads // lat
    place = col - (1 - core % 2) * (lon - per_row)
    return row * per_row + place, (place >= 0) & (place < per_row)


def steps_of(lat, lon, core):
    half = lon // 2
    found = [(True, row_step, 0) for row_step in range(lat - 1, -1, -1)]
    for row_step in range(lat - 1, -1, -1):
        for col_step in range(1, half):
            turns = (True, row_step, col_step), (False, row_step, col_step)
            found.extend(turns[::-1] if core % 2 else turns)
    found.extend((False, row_step, 0) for row_step in range(1, lat))
    return found + [(False, 0, 0)]


def column_after(col, step, lon):
    half = lon // 2
    other = col // half ^ int(step[0])
    return other * half + (col + step[2]) % half


def partner(row, col, core, n, lat, lon, back=False):
    places = []
    for which in (0, 1):
        step = steps_of(lat, lon, which)[n]
        to_row = lax.rem(row + (lat - step[1] if back else step[1]), lat)
        to_col = jnp.int32(0)
        for here in range(lon):
            there = column_after(here, step, lon)
            if back:
                to_col = jnp.where(col == there, here, to_col)
            else:
                to_col = jnp.where(col == here, there, to_col)
        places.append((to_row, to_col))
    return [jnp.where(core % 2 == 0, a, b) for a, b in zip(*places)]


def routes(n, lat, lon, cores, heads, back):
    pairs = []
    for row in range(lat):
        for col in range(lon):
            for core in range(cores):
                step = steps_of(lat, lon, core)[n]
                to_row, to_col = (row + step[1]) % lat, column_after(col, step, lon)
                if head_of(to_row, to_col, core, lat, lon, heads)[1]:
                    here = (col * lat + row) * cores + core
                    there = (to_col * lat + to_row) * cores + core
                    pairs.append((there, here) if back else (here, there))
    return pairs


def slot_counts(lat, lon):
    times = [[0] * (lat * lon) for _ in range(lat * lon)]
    for row in range(lat):
        for col in range(lon):
            for a in (-1, 0, 1):
                for b in (-1, 0, 1):
                    near_row, near_col = row + a, col + b
                    if near_row < 0 or near_row > lat - 1:
                        near_col += lon // 2
                        near_row = min(max(near_row, 0), lat - 1)
                    times[row * lon + col][near_row * lon + near_col % lon] += 1
    return times


def pack_kernel(lat, lon, heads, *refs):
    tensors, blocks, whole, sems = refs[:4], refs[4:-2], refs[-2], refs[-1]
    row, col, core = (lax.axis_index(a) for a in ("lat", "lon", "head"))
    parts = sems.shape[1]
    size = whole.shape[1] // parts
    copies = []
    for n in range(parts):
        rows = pl.ds(n * size, size)
        for t, tensor in enumerate(tensors):
            copies.append(
                pltpu.make_async_copy(
                    tensor.at[0, 0, rows, :], whole.at[t, rows, :], sems.at[t, n]
                )
            )
    for copy in copies:
        copy.start()
    for n in range(parts):
        rows = slice(n * size, (n + 1) * size)
        for copy in copies[4 * n : 4 * n + 4]:
            copy.wait()
        for m, block in enumerate(blocks):
            head, used = head_of(*partner(row, col, core, m, lat, lon), core, lat, lon, heads)

            @pl.when(used)
            def _():
                features = pl.ds(pl.multiple_of(head * HD, HD), HD)
                for t in range(4):
                    block[t, rows, :] = whole[t, rows, features]


def unpack_kernel(lat, lon, heads, *refs):
    blocks, tensors, whole, sems = refs[:-6], refs[-6:-2], refs[-2], refs[-1]
    row, col, core = (lax.axis_index(a) for a in ("lat", "lon", "head"))
    copies = []
    for t, tensor in enumerate(tensors):
        for m, block in enumerate(blocks):
            head, used = head_of(*partner(row, col, core, m, lat, lon), core, lat, lon, heads)

            @pl.when(used)
            def _():
                features = pl.ds(pl.multiple_of(head * HD, HD), HD)
                whole[t, :, features] = block[t]

        copies.append(pltpu.make_async_copy(whole.at[t], tensor.at[0, 0], sems.at[t]))
        copies[-1].start()
    for copy in copies:
        copy.wait()


class Sphere:
    def __init__(self, lat, lon, times, key_marks, query_marks):
        self.tiles = lat * lon
        self.times = times
        self.key_marks, self.query_marks = key_marks, query_marks
        self.size = key_marks.shape[1]
        self.wide = 2 * self.size
        self.rounds = self.tiles // 2
        self.scale = 1.0 / math.sqrt(HD)
        self.of_tile = lax.broadcasted_iota(jnp.int32, (1, self.wide), 1) // self.size
        self.held = [None] * self.tiles

    def mark(self, limits):
        shape = (self.size, HD)
        key_row = lax.broadcasted_iota(jnp.int32, shape, 0)
        lane = lax.broadcasted_iota(jnp.int32, shape, 1)
        for j in range(self.tiles):
            unseen = (lane == 0) & (key_row >= limits[j])
            key_mark = jnp.where(unseen, -1e30, jnp.where(lane == j + 1, 1.0, 0.0))
            self.key_marks[j] = key_mark.astype(self.key_marks.dtype)
            apart = jnp.zeros(shape, jnp.bool_)
            for k in range(self.tiles):
                if self.times[j][k] == 0:
                    apart = apart | (lane == k + 1)
            query_mark = jnp.where(apart, -1e30, jnp.where(lane == 0, 1.0, 0.0))
            self.query_marks[j] = query_mark.astype(self.query_marks.dtype)

    def rows(self, j):
        return slice(j * self.size, (j + 1) * self.size)

    def lanes(self, t):
        return slice(t * self.wide, (t + 1) * self.wide)

    def stacked(self, t, n):
        return jnp.concatenate([self.held[2 * t + k][n] for k in range(2)], 0)

    def marked(self, t, n, marks):
        parts = [(self.held[i][n], marks[i]) for i in (2 * t, 2 * t + 1)]
        return jnp.concatenate([jnp.concatenate(part, 1) for part in parts], 0)

    def score(self, t, u):
        return contract_last(
            self.marked(u, 1, self.key_marks), self.marked(t, 0, self.query_marks)
        )

    def grad_weight(self, t, u):
        return contract_last(self.stacked(u, 2), self.stacked(t, 3))

    def exponential(self, scores, top):
        return jnp.exp2((scores - top) * (self.scale * math.log2(math.e)))

    def named(self, t, j):
        line = jnp.ones((1, self.wide), jnp.float32)
        for k in range(2):
            if self.times[2 * t + k][j] > 1:
                line = jnp.where(self.of_tile == k, float(self.times[2 * t + k][j]), line)
        return line

    def folded(self, part, op):
        return op(part.reshape(part.shape[0] // 8, 8, self.wide), axis=0)

    def added(self, total, t, u, parts):
        for k in range(2):
            part = self.folded(parts[self.rows(k), :], jnp.sum) * self.named(t, 2 * u + k)
            total = part if total is None else total + part
        return total


def contract_last(a, b):
    return lax.dot_general(a, b, (((1,), (1,)), ((), ())), preferred_element_type=jnp.float32)


def greater(a, b):
    return b if a is None else jnp.maximum(a, b)


def begin_kernel(lat, lon, times, *refs):
    tiles = lat * lon
    all_counts, blocks, outs = refs[0], refs[1 : tiles - 1], refs[tiles - 1 :]
    key_marks, query_marks, keys_t, values_t, grads_t, scores, grad_weights, stats = outs[:8]
    counts, sem = outs[8:]
    sphere = Sphere(lat, lon, times, key_marks, query_marks)
    sphere.held[: tiles - 2] = blocks
    rounds = sphere.rounds - 1
    copy = pltpu.make_async_copy(all_counts, counts, sem)
    copy.start()
    for t in range(rounds):
        for u in range(rounds):
            grad_weights[t, sphere.lanes(u), :] = sphere.grad_weight(t, u)
        for i in (2 * t, 2 * t + 1):
            keys_t[:, sphere.rows(i)] = blocks[i][1].T
            values_t[:, sphere.rows(i)] = blocks[i][2].T
            grads_t[:, sphere.rows(i)] = blocks[i][3].T
    copy.wait()
    row, col, core = (lax.axis_index(a) for a in ("lat", "lon", "head"))
    limits = [
        counts[tuple(partner(row, col, core, n, lat, lon, True))] for n in range(tiles)
    ]
    sphere.mark(in_slots(limits))
    best, total = [None] * rounds, [None] * rounds

    def score(t, u):
        part = sphere.score(t, u)
        scores[t, sphere.lanes(u), :] = part
        best[t] = greater(best[t], sphere.folded(part, jnp.max))

    for u in range(rounds):
        score(0, u)
    for t in range(rounds):
        best[t] = jnp.max(best[t], axis=0, keepdims=True)
        for u in range(rounds):
            part = sphere.exponential(scores[t, sphere.lanes(u), :], best[t])
            scores[t, sphere.lanes(u), :] = part
            total[t] = sphere.added(total[t], t, u, part)
            if t + 1 < rounds:
                score(t + 1, u)
        stats[t, :8, :] = jnp.broadcast_to(best[t], (8, sphere.wide))
        stats[t, 8:, :] = total[t]


def finish_kernel(lat, lon, times, *refs):
    tiles = lat * lon
    blocks, refs = refs[:tiles], refs[tiles:]
    key_marks, query_marks, keys_t, values_t, grads_t, scores, grad_weights, stats = refs[:8]
    made, refs = refs[8 : 8 + tiles], refs[8 + tiles :]
    last_keys_t, last_values_t, last_grads_t, more_scores, weights_low, grads_low = refs
    sphere = Sphere(lat, lon, times, key_marks, query_marks)
    sphere.held[:] = blocks
    f32, low = jnp.float32, weights_low.dtype
    rounds, last = sphere.rounds, sphere.rounds - 1
    best, total, old, share, out_dot = ([None] * rounds for _ in range(5))
    early = slice(0, last * sphere.wide)
    late = sphere.lanes(last)

    def held_scores(t, j):
        if t < last and j // 2 < last:
            return scores.at[t, sphere.rows(j), :]
        if t < last:
            return more_scores.at[t, sphere.rows(j - 2 * last), :]
        return more_scores.at[last + j // 2, sphere.rows(j % 2), :]

    def score(t, u):
        part = sphere.score(t, u)
        for k in range(2):
            held_scores(t, 2 * u + k)[...] = part[sphere.rows(k), :]
        best[t] = greater(best[t], sphere.folded(part, jnp.max))

    def exponential(t, u):
        parts = []
        for j in (2 * u, 2 * u + 1):
            parts.append(sphere.exponential(held_scores(t, j)[...], best[t]))
            held_scores(t, j)[...] = parts[-1]
        total[t] = sphere.added(total[t], t, u, jnp.concatenate(parts, 0))

    def settle(t):
        before = stats[t, :1, :]
        best[t] = jnp.maximum(before, jnp.max(best[t], axis=0, keepdims=True))
        old[t] = sphere.exponential(before, best[t])
        total[t] = stats[t, 8:, :] * old[t]
        exponential(t, last)
        share[t] = 1.0 / jnp.sum(total[t], axis=0, keepdims=True)

    def factor(t, j):
        line = share[t] * sphere.named(t, j)
        return line * old[t] if t < last and j // 2 < last else line

    def weight(t, u):
        for j in (2 * u, 2 * u + 1):
            part = held_scores(t, j)[...] * factor(t, j)
            weights_low[sphere.rows(j), sphere.lanes(t)] = part.astype(low)

    def from_keys(first_t, last_t, low_scores, t):
        lanes = sphere.lanes(t)
        return jnp.dot(
            first_t[...], low_scores[early, lanes], preferred_element_type=f32
        ) + jnp.dot(last_t[...], low_scores[late, lanes], preferred_element_type=f32)

    def attend(t):
        out_t = from_keys(values_t, last_values_t, weights_low, t).astype(low)
        grad_t = grads_t[:, sphere.lanes(t)] if t < last else last_grads_t[...]
        out_dot[t] = jnp.sum(grad_t.astype(f32) * out_t.astype(f32), axis=0, keepdims=True)
        for k in range(2):
            made[2 * t + k][0] = out_t[:, sphere.rows(k)].T

    def grad_score(t, u):
        if t < last and u < last:
            part = grad_weights[t, sphere.lanes(u), :]
        else:
            part = sphere.grad_weight(t, u)
        for k in range(2):
            j = 2 * u + k
            weights = held_scores(t, j)[...] * factor(t, j)
            grad = weights * (part[sphere.rows(k), :] - out_dot[t])
            grads_low[sphere.rows(j), sphere.lanes(t)] = grad.astype(low)

    def query_grad(t):
        query_t = (from_keys(keys_t, last_keys_t, grads_low, t) * sphere.scale).astype(low)
        for k in range(2):
            made[2 * t + k][1] = query_t[:, sphere.rows(k)].T

    def key_side(n, low_scores, to, factor):
        part = jnp.dot(
            low_scores[...],
            jnp.concatenate([block[n] for block in blocks], 0),
            preferred_element_type=f32,
        )
        for j in range(tiles):
            made[j][to] = (part[sphere.rows(j), :] * factor).astype(low)

    for t in range(last):
        score(t, last)
    for k in range(2):
        block = blocks[2 * last + k]
        last_keys_t[:, sphere.rows(k)] = block[1].T
        last_values_t[:, sphere.rows(k)] = block[2].T
        last_grads_t[:, sphere.rows(k)] = block[3].T
    for t in range(last):
        settle(t)
        if t > 0:
            attend(t - 1)
        if t > 1:
            query_grad(t - 2)
        for u in range(rounds):
            weight(t, u)
            if t == 0:
                score(last, u)
            if t == 1 or last == 1:
                if u == 0:
                    best[last] = jnp.max(best[last], axis=0, keepdims=True)
                exponential(last, u)
            if t > 0:
                grad_score(t - 1, u)
    share[last] = 1.0 / jnp.sum(total[last], axis=0, keepdims=True)
    attend(last - 1)
    if last > 1:
        query_grad(last - 2)
    for u in range(rounds):
        weight(last, u)
        grad_score(last - 1, u)
    attend(last)
    key_side(3, weights_low, 3, 1.0)
    query_grad(last - 1)
    for u in range(rounds):
        grad_score(last, u)
    query_grad(last)
    key_side(0, grads_low, 2, sphere.scale)


def by_heads(queries, key_tokens, value_tokens, out_grad, counts):
    lat, lon, cores = (lax.axis_size(a) for a in ("lat", "lon", "head"))
    tiles = lat * lon
    tile_len, width = queries.shape[2], queries.shape[3]
    heads = width // HD
    low, f32 = queries.dtype, jnp.float32
    in_vmem = pl.BlockSpec(memory_space=pltpu.VMEM)
    in_hbm = pl.BlockSpec(memory_space=pltpu.HBM)
    whole = jax.ShapeDtypeStruct(queries.shape, low)
    block = pltpu.VMEM((4, tile_len, HD), low)
    small = pltpu.CompilerParams(vmem_limit_bytes=6 * 1024 * 1024)

    def sent(blocks, back):
        axes = ("lon", "lat", "head")
        moves = list(range(tiles - 1))
        if back:
            full, mixed, along = moves[:lat], moves[lat : 1 - lat], moves[1 - lat :]
            moves = full + mixed[::2] + mixed[1::2] + along
        found = list(blocks)
        for n in moves:
            found[n] = lax.ppermute(found[n], axes, routes(n, lat, lon, cores, heads, back))
        return found

    def from_hbm(*arrays):
        return [pltpu.with_memory_space_constraint(x, pltpu.HBM) for x in arrays]

    packed = pl.pallas_call(
        functools.partial(pack_kernel, lat, lon, heads),
        out_shape=[block] * tiles,
        in_specs=[in_hbm] * 4,
        out_specs=[in_vmem] * tiles,
        scratch_shapes=[
            pltpu.VMEM((4, tile_len, width), low),
            pltpu.SemaphoreType.DMA((4, 8)),
        ],
        compiler_params=small,
        name="pack",
    )(*from_hbm(queries, key_tokens, value_tokens, out_grad))
    there = in_slots(sent(packed, False))
    key_len, wide, begun = tiles * tile_len, 2 * tile_len, (tiles - 2) * tile_len
    times = relative_counts(lat, lon)
    large = pltpu.CompilerParams(vmem_limit_bytes=24 * 1024 * 1024)
    shared = [
        pltpu.VMEM((tiles, tile_len, HD), low),
        pltpu.VMEM((tiles, tile_len, HD), low),
        pltpu.VMEM((HD, begun), low),
        pltpu.VMEM((HD, begun), low),
        pltpu.VMEM((HD, begun), low),
        pltpu.VMEM((tiles // 2 - 1, begun, wide), f32),
        pltpu.VMEM((tiles // 2 - 1, begun, wide), f32),
        pltpu.VMEM((tiles // 2 - 1, 16, wide), f32),
    ]
    done = pl.pallas_call(
        functools.partial(begin_kernel, lat, lon, times),
        out_shape=shared,
        in_specs=[in_hbm] + [in_vmem] * (tiles - 2),
        out_specs=[in_vmem] * len(shared),
        scratch_shapes=[pltpu.SMEM(counts.shape, counts.dtype), pltpu.SemaphoreType.DMA],
        compiler_params=large,
        cost_estimate=pl.CostEstimate(
            flops=6 * begun * begun * HD,
            bytes_accessed=8 * begun * HD,
            transcendentals=begun * begun,
        ),
        name="begin",
    )(*from_hbm(counts), *there[: tiles - 2])
    made = pl.pallas_call(
        functools.partial(finish_kernel, lat, lon, times),
        out_shape=[block] * tiles,
        in_specs=[in_vmem] * (tiles + len(shared)),
        out_specs=[in_vmem] * tiles,
        scratch_shapes=[
            pltpu.VMEM((HD, wide), low),
            pltpu.VMEM((HD, wide), low),
            pltpu.VMEM((HD, wide), low),
            pltpu.VMEM((tiles - 1, wide, wide), f32),
            pltpu.VMEM((key_len, key_len), low),
            pltpu.VMEM((key_len, key_len), low),
        ],
        compiler_params=large,
        cost_estimate=pl.CostEstimate(
            flops=14 * key_len * key_len * HD - 6 * begun * begun * HD,
            bytes_accessed=16 * key_len * HD,
            transcendentals=key_len * key_len - begun * begun,
        ),
        name="finish",
    )(*there, *done)
    home = sent(in_steps(made), True)
    return tuple(
        pl.pallas_call(
            functools.partial(unpack_kernel, lat, lon, heads),
            out_shape=[whole] * 4,
            in_specs=[in_vmem] * tiles,
            out_specs=[in_hbm] * 4,
            scratch_shapes=[
                pltpu.VMEM((4, tile_len, width), low),
                pltpu.SemaphoreType.DMA((4,)),
            ],
            compiler_params=small,
            name="unpack",
        )(*home)
    )


def solution(mesh):
    tokens = P(("groups", "lat"), "lon", None, "head")

    def on_device(queries, *rest):
        lat, lon = mesh.shape["lat"], mesh.shape["lon"]
        one_tile = queries.shape[:2] == (1, 1)
        if one_tile and heads_fit(lat, lon, queries.shape[3] // HD):
            return by_heads(queries, *rest)
        return by_tiles(queries, *rest)

    return jax.shard_map(
        on_device,
        mesh=mesh,
        in_specs=(tokens,) * 4 + (P("groups", None),),
        out_specs=(tokens,) * 4,
        check_vma=False,
    )
```
